256 devices in a mesh: zonal: 16 (over y, x_hi, core), merid: 16 (over z, x_lo).
Axes of the slice: x: 4 (x_hi: 2, x_lo: 2; x = x_hi * 2 + x_lo), y: 4, z: 8, core: 2. Of those that a mesh axis runs over, the one named last changes fastest.
Arguments:
- tracers: float32 [2, 8, 128, 6144], P(None, None, 'merid', 'zonal'), may hold values from -6 to 6
- speed_east: float32 [8, 128, 6144], P(None, 'merid', 'zonal'), may hold values from -0.12 to 0.12
- speed_north: float32 [8, 128, 6144], P(None, 'merid', 'zonal'), may hold values from -0.12 to 0.12
- diff_horiz: float32 [8, 128, 6144], P(None, 'merid', 'zonal'), may hold values from 0.06 to 0.08
- diff_vert: float32 [8, 128, 6144], P(None, 'merid', 'zonal'), may hold values from 0.005 to 0.1
- sea_mask: int32 [8, 128, 6144], P(None, 'merid', 'zonal'), may hold values 0 or 1
Outputs:
- tracers_out: float32 [2, 8, 128, 6144], P(None, None, 'merid', 'zonal')
The draws below stay inside these ranges and needn't reach their ends.
Inputs may be any that keep to these rules, and one draw needn't show every extreme that they name: `sea_mask`: 1 marks a sea cell, 0 land.
All inputs are finite; a program needn't handle non-finite values. No bound on the sum of `sea_mask` on one device may be relied on, other than what follows from the above.
Results may differ from the reference program's by a relative error of at most 0.0001.
Values sent between devices are 32-bit elements; how exact they have to be, the bound alone decides.
No kernel may reach another device: no remote copies, remote signals or barrier semaphores. Data moves between devices by JAX's collectives and lax.ppermute only.
A program may use at most 192 MiB of HBM per device.

```python
import math
import jax
import jax.numpy as jnp

CX = 384
NZ = 8
STEPS = 6
ITERS = 2
NX = 6144
NY = 128
N_ZONAL = 16


def signed_speed(key, shape):
    first_key, second_key = jax.random.split(key)
    magnitude = jax.random.uniform(first_key, shape, jnp.float32, 0.09, 0.12)
    flipped = jax.random.bernoulli(second_key, 0.5, shape)
    return jnp.where(flipped, magnitude, -magnitude)


def draw_speed_east(key, part):
    key = jax.random.fold_in(key, 11)
    return signed_speed(key, (NZ, NY, NX))


def draw_speed_north(key, part):
    key = jax.random.fold_in(key, 23)
    return signed_speed(key, (NZ, NY, NX))


def set_ends(drawn, rng, low, high):
    extent = drawn.shape
    index_at = [jax.random.randint(jax.random.fold_in(rng, axis), (), 0, extent[axis]) for axis in range(len(extent))]
    drawn = drawn.at[tuple(index_at)].set(low)
    longest = extent.index(max(extent))
    index_at[longest] = (index_at[longest] + 1) % extent[longest]
    return drawn.at[tuple(index_at)].set(high)


def block_scale(key, extent, cuts, smallest, high):
    gain, own = 1.0, jax.random.fold_in(key, 6)
    for dim, shards_of in cuts:
        heights = jnp.exp(jax.random.uniform(jax.random.fold_in(own, dim), (shards_of,), jnp.float32, smallest / len(cuts), high / len(cuts)))
        gain = gain * jnp.repeat(heights, extent[dim] // shards_of).reshape([-1 if axis == dim else 1 for axis in range(len(extent))])
    return gain


def normal_values(stream_key, extent, spread, reach, shards=(), dtype=jnp.bfloat16):
    values = jax.random.normal(stream_key, extent, jnp.float32) * spread
    if len(shards) > 0:
        values = block_scale(stream_key, extent, shards, -0.22, 0.18) * values
    return jnp.clip(values, min=-reach, max=reach).astype(dtype)


def setup_inputs(seed: int = 0) -> dict:
    streams_of = jax.random.split(jax.random.key(seed), 7)
    tracers = normal_values(streams_of[0], (2, NZ, NY, NX), 1.0, 6.0, ((2, 16), (3, 16)), jnp.float32)
    speed_east = draw_speed_east(jax.random.fold_in(streams_of[6], 71), 0)
    speed_north = draw_speed_north(jax.random.fold_in(streams_of[6], 71), 0)
    diff_horiz = jnp.clip(0.06 + 0.02 * jax.random.uniform(streams_of[3], (NZ, NY, NX), jnp.float32) ** block_scale(streams_of[3], (NZ, NY, NX), ((1, 16), (2, 16)), -0.2, 0.2), 0.06, 0.08)
    diff_vert = jnp.clip(jnp.exp(math.log(0.1) - 2.9957323 * jax.random.uniform(streams_of[4], (NZ, NY, NX), jnp.float32) ** block_scale(streams_of[4], (NZ, NY, NX), ((1, 16), (2, 16)), -0.2, 0.2)), 0.005, 0.1)
    sea_mask = set_ends((jax.random.randint(streams_of[5], (NZ, NY, NX), 0, 8) < 7).astype(jnp.int32), jax.random.fold_in(streams_of[5], 1), 0, 1)
    return dict(tracers=tracers, speed_east=speed_east, speed_north=speed_north, diff_horiz=diff_horiz, diff_vert=diff_vert, sea_mask=sea_mask)


robin_weight = 0.5


def face_tables(coeffs):
    speed_east, speed_north, diff_horiz, diff_vert, sea_cells, speed_inlet, diff_inlet, sea_west, sea_east = coeffs
    face_speed = jnp.concatenate([speed_inlet[..., None], speed_east], axis=-1)
    face_diff = jnp.concatenate([diff_inlet[..., None], diff_horiz], axis=-1)
    sea_padded = jnp.concatenate([sea_west[..., None], sea_cells, sea_east[..., None]], axis=-1)
    face_sea = sea_padded[..., :-1] * sea_padded[..., 1:]
    zonal_left = (jnp.maximum(face_speed, 0.0) + face_diff) * face_sea
    zonal_right = (jnp.minimum(face_speed, 0.0) - face_diff) * face_sea
    sea_north = jnp.concatenate([sea_cells[:, 1:], jnp.zeros_like(sea_cells[:, :1])], axis=1)
    north_sea = sea_cells * sea_north
    merid_here = (jnp.maximum(speed_north, 0.0) + diff_horiz) * north_sea
    merid_there = (jnp.minimum(speed_north, 0.0) - diff_horiz) * north_sea
    sea_below = jnp.concatenate([sea_cells[1:], jnp.zeros_like(sea_cells[:1])], axis=0)
    vertical_coef = diff_vert * sea_cells * sea_below
    return (zonal_left, zonal_right, merid_here, merid_there, vertical_coef, sea_cells)


def transport_step(tracer, ghost_west, ghost_east, tables):
    zonal_left, zonal_right, merid_here, merid_there, vertical_coef, sea_cells = tables
    padded = jnp.concatenate([ghost_west[..., None], tracer, ghost_east[..., None]], axis=-1)
    zonal_flux = zonal_left * padded[..., :-1] + zonal_right * padded[..., 1:]
    zonal_div = zonal_flux[..., 1:] - zonal_flux[..., :-1]
    northern = jnp.concatenate([tracer[:, :, 1:], jnp.zeros_like(tracer[:, :, :1])], axis=2)
    merid_flux = merid_here * tracer + merid_there * northern
    merid_div = merid_flux - jnp.concatenate([jnp.zeros_like(merid_flux[:, :, :1]), merid_flux[:, :, :-1]], axis=2)
    lower_cell = jnp.concatenate([tracer[:, 1:], jnp.zeros_like(tracer[:, :1])], axis=1)
    vertical_flux = vertical_coef * (tracer - lower_cell)
    vertical_div = vertical_flux - jnp.concatenate([jnp.zeros_like(vertical_flux[:, :1]), vertical_flux[:, :-1]], axis=1)
    return sea_cells * (tracer - zonal_div - merid_div - vertical_div)


def reference(tracers, speed_east, speed_north, diff_horiz, diff_vert, sea_mask):
    def by_subdomain(array):
        return array.reshape(array.shape[:-1] + (N_ZONAL, CX))

    def from_west(array):
        return jnp.roll(array[..., -1], 1, axis=-1)

    def from_east(array):
        return jnp.roll(array[..., 0], -1, axis=-1)

    start = by_subdomain(tracers)
    speed_x = by_subdomain(speed_east)
    speed_y = by_subdomain(speed_north)
    diff_h = by_subdomain(diff_horiz)
    diff_v = by_subdomain(diff_vert)
    sea_cells = by_subdomain(sea_mask.astype(jnp.float32))
    coeffs = (speed_x, speed_y, diff_h, diff_v, sea_cells, from_west(speed_x), from_west(diff_h),
              from_west(sea_cells), from_east(sea_cells))
    tables = face_tables(coeffs)
    factor_a = 1.0 - robin_weight / 2.0
    factor_b = 1.0 + robin_weight / 2.0

    def solve(side_west, side_east, robin):
        current = start
        west_list = []
        east_list = []
        for moment in range(STEPS):
            first_col = current[..., 0]
            last_col = current[..., -1]
            if robin:
                ghost_west = (side_west[moment] + factor_a * first_col) / factor_b
                ghost_east = (side_east[moment] + factor_a * last_col) / factor_b
            else:
                ghost_west = side_west
                ghost_east = side_east
            west_list.append((first_col - ghost_west) + robin_weight * (first_col + ghost_west) / 2.0)
            east_list.append((last_col - ghost_east) + robin_weight * (last_col + ghost_east) / 2.0)
            current = transport_step(current, ghost_west, ghost_east, tables)
        return current, jnp.stack(west_list), jnp.stack(east_list)

    current, trace_west, trace_east = solve(from_west(start), from_east(start), False)
    for sweep in range(ITERS):
        current, trace_west, trace_east = solve(jnp.roll(trace_east, 1, axis=-1), jnp.roll(trace_west, -1, axis=-1), True)
    return current.reshape(tracers.shape)
```

```python
import jax
import jax.numpy as jnp
from jax import lax
from jax.experimental import pallas as pl
from jax.experimental.pallas import tpu as pltpu
from jax.sharding import PartitionSpec as P

STEPS = 6
HALO = 6
LANES = 128
EDGE = 8

ROBIN_WEIGHT = 0.5
FACTOR_A = 1.0 - ROBIN_WEIGHT / 2.0
FACTOR_B = 1.0 + ROBIN_WEIGHT / 2.0

U, V, K, KZ, M = 2, 3, 4, 5, 6
FIELDS = 7

TO_NORTH = [(f, r) for f in (0, 1, V, K, M) for r in range(2, 8)] + [
    (f, r) for f in (U, KZ) for r in range(3, 8)
]
TO_SOUTH = [(f, r) for f in (0, 1, M) for r in range(6)] + [
    (f, r) for f in (U, V, K, KZ) for r in range(5)
]


def lane_of():
    return lax.broadcasted_iota(jnp.int32, (8, LANES), 1)


def level_of():
    return lax.broadcasted_iota(jnp.int32, (8, LANES), 0)


def pack_kernel(tracers, speed_east, speed_north, diff_horiz, diff_vert, sea, own, north, south, edges):
    tiles = own.shape[-1] // LANES
    lane = lane_of()
    sources = (
        tracers.at[0],
        tracers.at[1],
        speed_east,
        speed_north,
        diff_horiz,
        diff_vert,
        sea,
    )
    for f, source in enumerate(sources):
        edge = jnp.zeros((8, LANES), jnp.float32)
        for r in range(8):
            for k in range(tiles):
                cols = pl.ds(k * LANES, LANES)
                value = source[pl.ds(8 * k + r, 8, stride=8 * tiles), :].astype(jnp.float32)
                own[f, r, :, cols] = value
                if (f, r) in TO_NORTH:
                    north[TO_NORTH.index((f, r)), :, cols] = value
                if (f, r) in TO_SOUTH:
                    south[TO_SOUTH.index((f, r)), :, cols] = value
                if k == 0:
                    shift = EDGE * r
                    moved = pltpu.roll(value, shift, 1) if shift else value
                    edge = jnp.where((lane >= shift) & (lane < shift + EDGE), moved, edge)
                if k == tiles - 1:
                    first = LANES // 2 + EDGE * r
                    shift = (first - (LANES - EDGE)) % LANES
                    moved = pltpu.roll(value, shift, 1) if shift else value
                    edge = jnp.where((lane >= first) & (lane < first + EDGE), moved, edge)
        edges[f] = edge


def solve_kernel(
    own, from_south, from_north, side_own, side_south, side_north, out,
    field, coef, state, strip, robin,
):
    width = own.shape[-1]
    tiles = width // LANES
    ring = tiles + 1
    rows = 8 + 2 * HALO
    lane = lane_of()
    level = level_of()
    first = lane == 0
    last = lane == LANES - 1
    low_half = lane < LANES // 2

    def west(value, beside):
        return pltpu.roll(jnp.where(last, beside, value), 1, 1)

    def east(value, beside):
        return pltpu.roll(jnp.where(first, beside, value), LANES - 1, 1)

    def across(value):
        return jnp.where(low_half, pltpu.roll(value, 1, 1), pltpu.roll(value, LANES - 1, 1))

    for f in range(FIELDS):
        for r in range(8):
            field[f, HALO + r, :, pl.ds(0, width)] = own[f, r]
    for i, (f, r) in enumerate(TO_NORTH):
        field[f, r - 2, :, pl.ds(0, width)] = from_south[i]
    for i, (f, r) in enumerate(TO_SOUTH):
        field[f, HALO + 8 + r, :, pl.ds(0, width)] = from_north[i]

    for f in range(FIELDS):
        for source, begin, shown in (
            (side_south, 2, 0),
            (side_own, 0, HALO),
            (side_north, 0, HALO + 8),
        ):
            packed = source[f]
            for i in range(8 if shown == HALO else HALO):
                r = begin + i
                low = pltpu.roll(packed, (LANES - EDGE * r) % LANES, 1) if r else packed
                shift = (LANES // 2 - EDGE * (r + 1)) % LANES
                high = pltpu.roll(packed, shift, 1) if shift else packed
                kept = jnp.where(lane < EDGE, low, jnp.where(lane >= LANES - EDGE, high, 0.0))
                field[f, shown + i, :, pl.ds(width, LANES)] = kept

    def get(ref, f, e, k):
        return ref[f, e, :, pl.ds((k % ring) * LANES, LANES)]

    def north_face(e, k):
        speed = get(field, V, e, k)
        diff = get(field, K, e, k)
        both = get(field, M, e, k) * get(field, M, e + 1, k)
        return (jnp.maximum(speed, 0.0) + diff) * both, (jnp.minimum(speed, 0.0) - diff) * both

    def table_row(e, carry):
        faces = []
        for k in range(ring):
            sea = get(field, M, e, k)
            both = sea * east(sea, get(field, M, e, k + 1))
            speed = get(field, U, e, k)
            diff = get(field, K, e, k)
            faces.append(
                ((jnp.maximum(speed, 0.0) + diff) * both, (jnp.minimum(speed, 0.0) - diff) * both)
            )
        for k in range(ring):
            here, there = faces[k]
            here_west = west(here, faces[k - 1][0])
            there_west = west(there, faces[k - 1][1])
            north_here, north_there = north_face(e, k)
            south_here, south_there = north_face(e - 1, k)
            sea = get(field, M, e, k)
            beneath = jnp.where(level == 7, 0.0, pltpu.roll(sea, 7, 0))
            below = get(field, KZ, e, k) * sea * beneath
            above = pltpu.roll(below, 1, 0)
            centre = sea - (
                here - there_west + north_here - south_there + below + above
            )
            cols = pl.ds(k * LANES, LANES)
            for i, value in enumerate(
                (centre, -there, here_west, -north_there, south_here, below, above)
            ):
                coef[i, e, :, cols] = value
        return carry

    lax.fori_loop(1, rows - 1, table_row, 0)

    def stencil(weights, value, to_east, to_west, to_north, to_south):
        centre, w_east, w_west, w_north, w_south, w_below, w_above = weights
        return (
            (centre * value + w_east * to_east)
            + (w_west * to_west + w_north * to_north)
            + (w_south * to_south + w_below * pltpu.roll(value, 7, 0))
            + w_above * pltpu.roll(value, 1, 0)
        )

    def side_weights(e, i):
        return jnp.where(low_half, get(coef, i, e, 0), get(coef, i, e, tiles - 1))

    def fill(e, carry):
        for t in range(2):
            strip[0, 0, t, e] = jnp.where(low_half, get(field, t, e, 0), get(field, t, e, tiles - 1))
            strip[1, 0, t, e] = get(field, t, e, tiles)
        return carry

    lax.fori_loop(1, rows - 1, fill, 0)

    for n in range(STEPS):
        now, later = n % 2, (n + 1) % 2

        def traces(e, carry, n=n, now=now):
            for t in range(2):
                mine = strip[0, now, t, e]
                ghost = across(get(field, t, e, tiles))
                told = across(FACTOR_B * mine - FACTOR_A * ghost)
                theirs = strip[1, now, t, e]
                ghost = (told + FACTOR_A * theirs) * (1.0 / FACTOR_B)
                robin[0, n, t, e] = ghost
                robin[1, n, t, e] = across(FACTOR_B * theirs - FACTOR_A * ghost) * (1.0 / FACTOR_B)
            return carry

        lax.fori_loop(1 + n, rows - 1 - n, traces, 0, unroll=2)
        if n == STEPS - 1:
            break

        def advance(e, carry, n=n, now=now, later=later):
            own_weights = [side_weights(e, i) for i in range(7)]
            side = [get(coef, i, e, tiles) for i in range(7)]
            for t in range(2):
                mine = strip[0, now, t, e]
                beside = get(field, t, e, tiles)
                strip[0, later, t, e] = stencil(
                    own_weights, mine, east(mine, beside), west(mine, beside),
                    strip[0, now, t, e + 1], strip[0, now, t, e - 1],
                )
                theirs = strip[1, now, t, e]
                ghost = robin[0, n, t, e]
                strip[1, later, t, e] = stencil(
                    side, theirs,
                    jnp.where(last, ghost, pltpu.roll(theirs, LANES - 1, 1)),
                    jnp.where(first, ghost, pltpu.roll(theirs, 1, 1)),
                    strip[1, now, t, e + 1], strip[1, now, t, e - 1],
                )
            return carry

        lax.fori_loop(2 + n, rows - 2 - n, advance, 0, unroll=2)

    for n in range(STEPS):
        def sweep(e, carry, n=n):
            source = (lambda t, e, k: get(field, t, e, k)) if n == 0 else (
                lambda t, e, k: state[n % 2, t, e, :, pl.ds(k * LANES, LANES)]
            )
            for k in range(tiles):
                weights = [get(coef, i, e, k) for i in range(7)]
                for t in range(2):
                    value = source(t, e, k)
                    if k == 0:
                        ghost = robin[1, n, t, e] + (FACTOR_A / FACTOR_B) * value
                        to_west = jnp.where(first, ghost, pltpu.roll(value, 1, 1))
                    else:
                        to_west = west(value, source(t, e, k - 1))
                    if k == tiles - 1:
                        ghost = robin[1, n, t, e] + (FACTOR_A / FACTOR_B) * value
                        to_east = jnp.where(last, ghost, pltpu.roll(value, LANES - 1, 1))
                    else:
                        to_east = east(value, source(t, e, k + 1))
                    stepped = stencil(
                        weights, value, to_east, to_west, source(t, e + 1, k), source(t, e - 1, k)
                    )
                    cols = pl.ds(k * LANES, LANES)
                    if n == STEPS - 1:
                        out[t, pl.ds(8 * k + e - HALO, 8, stride=8 * tiles), :] = stepped
                    else:
                        state[(n + 1) % 2, t, e, :, cols] = stepped
            return carry

        if n == STEPS - 1:
            for e in range(HALO, HALO + 8):
                sweep(e, 0)
        else:
            lax.fori_loop(1 + n, rows - 1 - n, sweep, 0, unroll=2)


def in_vmem(count):
    return [pl.BlockSpec(memory_space=pltpu.VMEM)] * count


def in_tiles(array):
    lead = array.shape[:-2]
    tiled = array.reshape(lead + (8, -1, LANES))
    return jnp.swapaxes(tiled, -3, -2).reshape(lead[:-1] + (-1, LANES))


def from_tiles(array, shape):
    tiled = array.reshape(shape[:-2] + (-1, 8, LANES))
    return jnp.swapaxes(tiled, -3, -2).reshape(shape)


def shards(tracers, speed_east, speed_north, diff_horiz, diff_vert, sea_mask):
    shape = tracers.shape
    width = shape[-1]
    rows = 8 + 2 * HALO
    f32 = jnp.float32
    flat = [
        in_tiles(a) for a in (tracers, speed_east, speed_north, diff_horiz, diff_vert, sea_mask)
    ]
    own, north, south, edges = pl.pallas_call(
        pack_kernel,
        out_shape=(
            jax.ShapeDtypeStruct((FIELDS, 8, 8, width), f32),
            jax.ShapeDtypeStruct((len(TO_NORTH), 8, width), f32),
            jax.ShapeDtypeStruct((len(TO_SOUTH), 8, width), f32),
            jax.ShapeDtypeStruct((FIELDS, 8, LANES), f32),
        ),
        in_specs=in_vmem(6),
        out_specs=tuple(in_vmem(4)),
        name="pack",
    )(*flat)

    count_m = lax.axis_size("merid")
    up = [(i, i + 1) for i in range(count_m - 1)]
    down = [(b, a) for a, b in up]
    count_z = lax.axis_size("zonal")
    onward = [(i, (i + 1) % count_z) for i in range(count_z)]
    back = [(b, a) for a, b in onward]

    from_south = lax.ppermute(north, "merid", up)
    from_north = lax.ppermute(south, "merid", down)
    from_west = lax.ppermute(edges, "zonal", onward)
    from_east = lax.ppermute(edges, "zonal", back)
    lane = lax.broadcasted_iota(jnp.int32, edges.shape, 2)
    side_own = jnp.where(lane < LANES // 2, from_east, from_west)
    side_south = lax.ppermute(side_own, "merid", up)
    side_north = lax.ppermute(side_own, "merid", down)

    ring = width + LANES
    result = pl.pallas_call(
        solve_kernel,
        out_shape=jax.ShapeDtypeStruct(flat[0].shape, f32),
        in_specs=in_vmem(6),
        out_specs=in_vmem(1)[0],
        scratch_shapes=[
            pltpu.VMEM((FIELDS, rows, 8, ring), f32),
            pltpu.VMEM((7, rows, 8, ring), f32),
            pltpu.VMEM((2, 2, rows, 8, width), f32),
            pltpu.VMEM((2, 2, 2, rows, 8, LANES), f32),
            pltpu.VMEM((2, STEPS, 2, rows, 8, LANES), f32),
        ],
        compiler_params=pltpu.CompilerParams(vmem_limit_bytes=24 * 1024 * 1024),
        name="solve",
    )(own, from_south, from_north, side_own, side_south, side_north)
    return from_tiles(result, shape)


def solution(mesh):
    row = P(None, "merid", "zonal")
    whole = P(None, None, "merid", "zonal")
    return jax.shard_map(
        shards, mesh=mesh, in_specs=(whole, row, row, row, row, row), out_specs=whole, check_vma=False
    )
```

```python
import jax
import jax.numpy as jnp
from jax import lax
from jax.experimental import pallas as pl
from jax.experimental.pallas import tpu as pltpu
from jax.sharding import PartitionSpec as P

STEPS = 6
LANES = 128
ROWS = 8

ROBIN_WEIGHT = 0.5
FACTOR_A = 1.0 - ROBIN_WEIGHT / 2.0
FACTOR_B = 1.0 + ROBIN_WEIGHT / 2.0

U, V, K, KZ, M = 2, 3, 4, 5, 6
FIELDS = 7

TO_SOUTH = (
    [(0, t, r) for t in (0, 1) for r in (0, 1)]
    + [(1, t, r) for t in (0, 1) for r in (1, 2)]
    + [(2, t, r) for t in (0, 1) for r in (2, 3)]
    + [(0, f, r) for f in (U, V, K, KZ) for r in (0, 1, 2)]
    + [(0, M, r) for r in (0, 1, 2, 3)]
)
TO_NORTH = (
    [(0, t, r) for t in (0, 1) for r in (6, 7)]
    + [(1, t, r) for t in (0, 1) for r in (5, 6)]
    + [(2, t, r) for t in (0, 1) for r in (4, 5)]
    + [(0, f, r) for f in (U, KZ) for r in (5, 6, 7)]
    + [(0, f, r) for f in (V, K, M) for r in (4, 5, 6, 7)]
)
BORDER = 4

COLS = 6
RIM = 6
OWN_LANE = COLS * RIM

STRIPS_TO_SOUTH = ((36, 32, 0, 84), (36, 36, 32, 84), (36, 25, 68, 84), (36, 30, 93, 84))
STRIPS_TO_NORTH = ((48, 36, 0, 0), (52, 32, 36, 4), (54, 30, 68, 6), (59, 25, 98, 11))


def lanes():
    return lax.broadcasted_iota(jnp.int32, (8, LANES), 1)


def turn(value, shift):
    shift = shift % LANES
    return pltpu.roll(value, shift, 1) if shift else value


def upward(value):
    return pltpu.roll(value, 7, 0)


def downward(value):
    return pltpu.roll(value, 1, 0)


def west(value, beside):
    return turn(jnp.where(lanes() == LANES - 1, beside, value), 1)


def east(value, beside):
    return turn(jnp.where(lanes() == 0, beside, value), -1)


def face(speed, diff, both):
    return (jnp.maximum(speed, 0.0) + diff) * both, (jnp.minimum(speed, 0.0) - diff) * both


def vertical(diff, sea):
    level = lax.broadcasted_iota(jnp.int32, (8, LANES), 0)
    below = diff * sea * jnp.where(level == 7, 0.0, upward(sea))
    return below, downward(below)


def collected(sea, faces_east, faces_west, faces_north, faces_south, faces_vertical):
    here, there = faces_east
    here_west, there_west = faces_west
    north_here, north_there = faces_north
    south_here, south_there = faces_south
    below, above = faces_vertical
    centre = sea - ((here - there_west) + (north_here - south_there) + (below + above))
    return centre, -there, here_west, -north_there, south_here, below, above


def stencil(weights, value, to_east, to_west, to_north, to_south):
    centre, w_east, w_west, w_north, w_south, w_below, w_above = weights
    return (
        (centre * value + (w_north * to_north + w_south * to_south))
        + (w_below * upward(value) + w_above * downward(value))
        + (w_east * to_east + w_west * to_west)
    )


def north_faces(get, r, tiles):
    return [
        face(get(V, r, k), get(K, r, k), get(M, r, k) * get(M, r + 1, k)) for k in range(tiles)
    ]


def row_weights(get, r, tiles, faces_north, faces_south, interface=None):
    sea = [get(M, r, k) for k in range(tiles)]
    faces = []
    for k in range(tiles):
        both = sea[k] * (east(sea[k], sea[k + 1]) if k + 1 < tiles else turn(sea[k], -1))
        faces.append(face(get(U, r, k), get(K, r, k), both))
    ends = faces[-1]
    if interface is not None:
        at_end = lanes() == LANES - 1
        faces[-1] = tuple(jnp.where(at_end, i, e) for i, e in zip(interface, ends))
        ends = tuple(jnp.where(at_end, turn(i, -1), e) for i, e in zip(interface, ends))
    weights = []
    for k in range(tiles):
        before = faces[k - 1] if k else ends
        faces_west = tuple(west(v, b) for v, b in zip(faces[k], before))
        faces_vertical = vertical(get(KZ, r, k), sea[k])
        weights.append(
            collected(sea[k], faces[k], faces_west, faces_north[k], faces_south[k], faces_vertical)
        )
    return weights


def pack_kernel(
    tracers, speed_east, speed_north, diff_horiz, diff_vert, sea,
    own, firsts, lasts, loaded, loaded_sea, sems,
):
    tiles = own.shape[-1] // LANES
    lane = lanes()
    sources = (tracers.at[0], tracers.at[1], speed_east, speed_north, diff_horiz, diff_vert, sea)
    copies = [
        pltpu.make_async_copy(source, loaded_sea if f == M else loaded.at[f], sems.at[f])
        for f, source in enumerate(sources)
    ]
    for copy in copies:
        copy.start()

    for f in range(FIELDS):
        copies[f].wait()
        source = loaded_sea if f == M else loaded.at[f]
        first_cols = jnp.zeros((8, LANES), jnp.float32)
        last_cols = first_cols
        for r in range(ROWS):
            begin = OWN_LANE + COLS * r
            here = (lane >= begin) & (lane < begin + COLS)
            for k in range(tiles):
                value = source[pl.ds(8 * k + r, 8, stride=8 * tiles), :].astype(jnp.float32)
                own[f, r, :, pl.ds(k * LANES, LANES)] = value
                if k == 0:
                    first_cols = jnp.where(here, turn(value, begin), first_cols)
                if k == tiles - 1:
                    last_cols = jnp.where(here, turn(value, begin + COLS), last_cols)
        firsts[f] = first_cols
        lasts[f] = last_cols


def border_kernel(own, firsts, lasts, from_east, from_west, north, south, coef, state):
    tiles = own.shape[-1] // LANES
    lane = lanes()

    def put(item, k, value):
        if item in TO_NORTH:
            north[TO_NORTH.index(item) * tiles + k] = value
        if item in TO_SOUTH:
            south[TO_SOUTH.index(item) * tiles + k] = value

    def get(f, r, k):
        return own[f, r, :, pl.ds(k * LANES, LANES)]

    for f in range(FIELDS):
        for r in range(ROWS):
            for k in range(tiles):
                put((0, f, r), k, get(f, r, k))

    faces = [north_faces(get, r, tiles) for r in range(0, ROWS - 1)]
    for r in range(1, ROWS - 1):
        weights = row_weights(get, r, tiles, faces[r], faces[r - 1])
        for k in range(tiles):
            cols = pl.ds(k * LANES, LANES)
            for i in range(7):
                coef[i, r, :, cols] = weights[k][i]

    for n in range(2):
        def read(t, r, k, n=n):
            return get(t, r, k) if n == 0 else state[t, r, :, pl.ds(k * LANES, LANES)]

        for r in range(1 + n, ROWS - 1 - n):
            for k in range(tiles):
                cols = pl.ds(k * LANES, LANES)
                weights = [coef[i, r, :, cols] for i in range(7)]
                for t in range(2):
                    value = read(t, r, k)
                    stepped = stencil(
                        weights,
                        value,
                        east(value, read(t, r, k + 1)) if k + 1 < tiles else turn(value, -1),
                        west(value, read(t, r, k - 1)) if k else turn(value, 1),
                        read(t, r + 1, k),
                        read(t, r - 1, k),
                    )
                    if n == 0:
                        state[t, r, :, cols] = stepped
                    put((n + 1, t, r), k, stepped)

    for out, items, pieces in ((north, TO_NORTH, STRIPS_TO_NORTH), (south, TO_SOUTH, STRIPS_TO_SOUTH)):
        for f in range(FIELDS):
            message = jnp.zeros((8, LANES), jnp.float32)
            for strip, (begin, length, there, _) in zip((firsts, lasts, from_east, from_west), pieces):
                moved = turn(strip[f], there - begin)
                message = jnp.where((lane >= there) & (lane < there + length), moved, message)
            out[len(items) * tiles + f] = message


def solve_kernel(
    own, from_south, from_north, firsts, lasts, east_firsts, west_lasts, out, field, coef, state,
):
    tiles = own.shape[-1] // LANES
    lane = lanes()
    column = lax.rem(lane, COLS)
    at_first = column == 0
    at_last = column == COLS - 1

    def assembled(which, source):
        fields = []
        for f in range(FIELDS):
            value = source[f]
            for message, items, pieces in (
                (from_south, TO_NORTH, STRIPS_TO_NORTH),
                (from_north, TO_SOUTH, STRIPS_TO_SOUTH),
            ):
                _, length, there, begin = pieces[which]
                moved = turn(message[len(items) * tiles + f], begin - there)
                value = jnp.where((lane >= begin) & (lane < begin + length), moved, value)
            fields.append(value)
        return fields

    own_first = assembled(0, firsts)
    own_last = assembled(1, lasts)
    east_first = assembled(2, east_firsts)
    west_last = assembled(3, west_lasts)

    def to_first(value):
        return turn(value, 1 - COLS)

    def to_last(value):
        return turn(value, COLS - 1)

    def strip_weights(left, right):
        both = left[M] * jnp.where(at_last, to_last(right[M]), turn(left[M], -1))
        left_faces = face(left[U], left[K], both)
        right_faces = face(right[U], right[K], right[M] * turn(right[M], -1))
        left_west = tuple(turn(v, 1) for v in left_faces)
        right_west = tuple(
            jnp.where(at_first, to_first(l), turn(v, 1)) for l, v in zip(left_faces, right_faces)
        )
        weights = []
        for strip, faces, faces_west in ((left, left_faces, left_west), (right, right_faces, right_west)):
            north = face(strip[V], strip[K], strip[M] * turn(strip[M], -COLS))
            south = tuple(turn(v, COLS) for v in north)
            weights.append(
                collected(strip[M], faces, faces_west, north, south, vertical(strip[KZ], strip[M]))
            )
        return weights[0], weights[1], left_faces

    w_west_last, w_own_first, west_face = strip_weights(west_last, own_first)
    w_own_last, w_east_first, east_face = strip_weights(own_last, east_first)

    def step_first(weights, value, ghost):
        return stencil(
            weights, value, turn(value, -1), jnp.where(at_first, ghost, turn(value, 1)),
            turn(value, -COLS), turn(value, COLS),
        )

    def step_last(weights, value, ghost):
        return stencil(
            weights, value, jnp.where(at_last, ghost, turn(value, -1)), turn(value, 1),
            turn(value, -COLS), turn(value, COLS),
        )

    def trace(value, ghost):
        return FACTOR_B * value - FACTOR_A * ghost

    def robin(told, value):
        return (told + FACTOR_A * value) * (1.0 / FACTOR_B)

    ghosts = []
    first_steps = []
    last_steps = []
    for t in range(2):
        ghost_first = to_first(west_last[t])
        ghost_last = to_last(east_first[t])
        a_first, a_last = own_first[t], own_last[t]
        b_first, b_last = east_first[t], west_last[t]
        c_first, c_last = own_first[t], own_last[t]
        ghosts_t = []
        steps_first, steps_last = [], []
        for n in range(STEPS):
            told_last = to_last(trace(a_first, ghost_first))
            told_first = to_first(trace(a_last, ghost_last))
            robin_last = robin(told_last, b_last)
            robin_first = robin(told_first, b_first)
            trace_last = trace(b_last, robin_last)
            trace_first = trace(b_first, robin_first)
            ghosts_t.append(
                jnp.where(at_last, trace_last, turn(trace_first, COLS - 2)) * (1.0 / FACTOR_B)
            )
            if n < STEPS - 1:
                a_first = step_first(w_own_first, a_first, ghost_first)
                a_last = step_last(w_own_last, a_last, ghost_last)
                b_first = step_first(w_east_first, b_first, robin_first)
                b_last = step_last(w_west_last, b_last, robin_last)
            if n < 2:
                c_first = step_first(w_own_first, c_first, robin(to_first(trace_last), c_first))
                c_last = step_last(w_own_last, c_last, robin(to_last(trace_first), c_last))
                steps_first.append(c_first)
                steps_last.append(c_last)
        ghosts.append(ghosts_t)
        first_steps.append(steps_first)
        last_steps.append(steps_last)

    def ends_of(value, r):
        return turn(value, -(COLS * (r + RIM) + COLS - 1))

    faces_at_ends = [
        jnp.where(at_last, w, turn(e, -1)) for w, e in zip(west_face, east_face)
    ]

    def cols(k):
        return pl.ds(k * LANES, LANES)

    for source, items, offset in ((from_south, TO_NORTH, -ROWS), (from_north, TO_SOUTH, ROWS)):
        for i, (n, f, r) in enumerate(items):
            r = r + offset
            for k in range(tiles):
                value = source[i * tiles + k]
                if n and k == 0:
                    fixed = turn(first_steps[f][n - 1], -COLS * (r + RIM))
                    value = jnp.where(lane < n, fixed, value)
                if n and k == tiles - 1:
                    fixed = turn(last_steps[f][n - 1], -COLS * (r + RIM + 1))
                    value = jnp.where(lane >= LANES - n, fixed, value)
                if f < 2:
                    state[n % 2, f, r + BORDER, :, cols(k)] = value
                else:
                    field[f, r + BORDER, :, cols(k)] = value

    def get(f, r, k):
        if 0 <= r < ROWS:
            return own[f, r, :, cols(k)]
        return field[f, r + BORDER, :, cols(k)]

    def read(n, t, r, k):
        if n == 0 and 0 <= r < ROWS:
            return own[t, r, :, cols(k)]
        return state[n % 2, t, r + BORDER, :, cols(k)]

    reach = BORDER - 1
    faces_south = north_faces(get, -reach - 1, tiles)
    for r in range(-reach, ROWS + reach):
        faces_north = north_faces(get, r, tiles)
        interface = tuple(ends_of(v, r) for v in faces_at_ends)
        weights = row_weights(get, r, tiles, faces_north, faces_south, interface)
        faces_south = faces_north
        for k in range(tiles):
            for i in range(7):
                coef[i, r + BORDER, :, cols(k)] = weights[k][i]

    for n in range(STEPS):
        more = min(n + 1, STEPS - 1 - n)
        for r in range(-more, ROWS + more):
            ends = [ends_of(ghosts[t][n], r) for t in range(2)]
            for k in range(tiles):
                weights = [coef[i, r + BORDER, :, cols(k)] for i in range(7)]
                for t in range(2):
                    value = read(n, t, r, k)
                    if k == 0 or k == tiles - 1:
                        ghost = ends[t] + (FACTOR_A / FACTOR_B) * value
                    if k == 0:
                        to_west = jnp.where(lane == 0, ghost, turn(value, 1))
                    else:
                        to_west = west(value, read(n, t, r, k - 1))
                    if k == tiles - 1:
                        to_east = jnp.where(lane == LANES - 1, ghost, turn(value, -1))
                    else:
                        to_east = east(value, read(n, t, r, k + 1))
                    stepped = stencil(
                        weights, value, to_east, to_west, read(n, t, r + 1, k), read(n, t, r - 1, k)
                    )
                    if n == STEPS - 1:
                        out[t, pl.ds(8 * k + r, 8, stride=8 * tiles), :] = stepped
                    else:
                        state[(n + 1) % 2, t, r + BORDER, :, cols(k)] = stepped


def granted(mib=16):
    return pltpu.CompilerParams(vmem_limit_bytes=mib * 1024 * 1024)


def in_vmem(count):
    return [pl.BlockSpec(memory_space=pltpu.VMEM)] * count


def in_tiles(array):
    lead = array.shape[:-2]
    tiled = array.reshape(lead + (8, -1, LANES))
    return jnp.swapaxes(tiled, -3, -2).reshape(lead[:-1] + (-1, LANES))


def from_tiles(array, shape):
    tiled = array.reshape(shape[:-2] + (-1, 8, LANES))
    return jnp.swapaxes(tiled, -3, -2).reshape(shape)


def pack(*arrays):
    f32 = jnp.float32
    width = arrays[1].size // 64
    return pl.pallas_call(
        pack_kernel,
        out_shape=(
            jax.ShapeDtypeStruct((FIELDS, ROWS, 8, width), f32),
            jax.ShapeDtypeStruct((FIELDS, 8, LANES), f32),
            jax.ShapeDtypeStruct((FIELDS, 8, LANES), f32),
        ),
        in_specs=[pl.BlockSpec(memory_space=pltpu.HBM)] * 6,
        out_specs=tuple(in_vmem(3)),
        scratch_shapes=[
            pltpu.VMEM((M,) + arrays[1].shape, f32),
            pltpu.VMEM(arrays[5].shape, arrays[5].dtype),
            pltpu.SemaphoreType.DMA((FIELDS,)),
        ],
        compiler_params=granted(),
        name="pack",
    )(*arrays)


def border(own, *strips):
    f32 = jnp.float32
    width = own.shape[-1]
    tiles = width // LANES
    return pl.pallas_call(
        border_kernel,
        out_shape=(
            jax.ShapeDtypeStruct((len(TO_NORTH) * tiles + FIELDS, 8, LANES), f32),
            jax.ShapeDtypeStruct((len(TO_SOUTH) * tiles + FIELDS, 8, LANES), f32),
        ),
        in_specs=in_vmem(5),
        out_specs=tuple(in_vmem(2)),
        scratch_shapes=[
            pltpu.VMEM((7, ROWS, 8, width), f32),
            pltpu.VMEM((2, ROWS, 8, width), f32),
        ],
        compiler_params=granted(),
        name="border",
    )(own, *strips)


def solve(own, *others):
    f32 = jnp.float32
    width = own.shape[-1]
    rows = ROWS + 2 * BORDER
    return pl.pallas_call(
        solve_kernel,
        out_shape=jax.ShapeDtypeStruct((2, width // LANES * 64, LANES), f32),
        in_specs=in_vmem(7),
        out_specs=in_vmem(1)[0],
        scratch_shapes=[
            pltpu.VMEM((FIELDS, rows, 8, width), f32),
            pltpu.VMEM((7, rows, 8, width), f32),
            pltpu.VMEM((2, 2, rows, 8, width), f32),
        ],
        compiler_params=granted(),
        name="solve",
    )(own, *others)


def shards(tracers, speed_east, speed_north, diff_horiz, diff_vert, sea_mask):
    arrays = (tracers, speed_east, speed_north, diff_horiz, diff_vert, sea_mask)
    own, firsts, lasts = pack(
        *[pltpu.with_memory_space_constraint(in_tiles(a), pltpu.HBM) for a in arrays]
    )

    count_m = lax.axis_size("merid")
    up = [(i, i + 1) for i in range(count_m - 1)]
    down = [(b, a) for a, b in up]
    count_z = lax.axis_size("zonal")
    onward = [(i, (i + 1) % count_z) for i in range(count_z)]
    back = [(b, a) for a, b in onward]

    from_west = lax.ppermute(lasts, "zonal", onward)
    from_east = lax.ppermute(firsts, "zonal", back)
    north, south = border(own, firsts, lasts, from_east, from_west)
    from_south = lax.ppermute(north, "merid", up)
    from_north = lax.ppermute(south, "merid", down)
    result = solve(own, from_south, from_north, firsts, lasts, from_east, from_west)
    return from_tiles(result, tracers.shape)


def solution(mesh):
    row = P(None, "merid", "zonal")
    whole = P(None, None, "merid", "zonal")
    return jax.shard_map(
        shards, mesh=mesh, in_specs=(whole, row, row, row, row, row), out_specs=whole, check_vma=False
    )
```

```python
import jax
import jax.numpy as jnp
from jax import lax
from jax.experimental import pallas as pl
from jax.experimental.pallas import tpu as pltpu
from jax.sharding import PartitionSpec as P

STEPS = 6
LANES = 128
ROWS = 8

ROBIN_WEIGHT = 0.5
FACTOR_A = 1.0 - ROBIN_WEIGHT / 2.0
FACTOR_B = 1.0 + ROBIN_WEIGHT / 2.0

U, V, K, KZ, M = 2, 3, 4, 5, 6
FIELDS = 7

TO_SOUTH = (
    [(0, t, r) for t in (0, 1) for r in (0, 1)]
    + [(1, t, r) for t in (0, 1) for r in (1, 2)]
    + [(2, t, r) for t in (0, 1) for r in (2, 3)]
    + [(0, f, r) for f in (U, V, K, KZ) for r in (0, 1, 2)]
    + [(0, M, r) for r in (0, 1, 2, 3)]
)
TO_NORTH = (
    [(0, t, r) for t in (0, 1) for r in (6, 7)]
    + [(1, t, r) for t in (0, 1) for r in (5, 6)]
    + [(2, t, r) for t in (0, 1) for r in (4, 5)]
    + [(0, f, r) for f in (U, KZ) for r in (5, 6, 7)]
    + [(0, f, r) for f in (V, K, M) for r in (4, 5, 6, 7)]
)
BORDER = 4

COLS = 6
RIM = 6
OWN_LANE = COLS * RIM

STRIPS_TO_SOUTH = ((36, 32, 0, 84), (36, 36, 32, 84), (36, 25, 68, 84), (36, 30, 93, 84))
STRIPS_TO_NORTH = ((48, 36, 0, 0), (52, 32, 36, 4), (54, 30, 68, 6), (59, 25, 98, 11))


def lanes():
    return lax.broadcasted_iota(jnp.int32, (8, LANES), 1)


def is_even(axis):
    return lax.rem(lax.axis_index(axis), 2) == 0


def turn(value, shift):
    shift = shift % LANES
    return pltpu.roll(value, shift, 1) if shift else value


def upward(value):
    return pltpu.roll(value, 7, 0)


def downward(value):
    return pltpu.roll(value, 1, 0)


def west(value, beside):
    return turn(jnp.where(lanes() == LANES - 1, beside, value), 1)


def east(value, beside):
    return turn(jnp.where(lanes() == 0, beside, value), -1)


def face(speed, diff, both):
    return (jnp.maximum(speed, 0.0) + diff) * both, (jnp.minimum(speed, 0.0) - diff) * both


def vertical(diff, sea):
    level = lax.broadcasted_iota(jnp.int32, (8, LANES), 0)
    below = diff * sea * jnp.where(level == 7, 0.0, upward(sea))
    return below, downward(below)


def collected(sea, faces_east, faces_west, faces_north, faces_south, faces_vertical):
    here, there = faces_east
    here_west, there_west = faces_west
    north_here, north_there = faces_north
    south_here, south_there = faces_south
    below, above = faces_vertical
    centre = sea - ((here - there_west) + (north_here - south_there) + (below + above))
    return centre, -there, here_west, -north_there, south_here, below, above


def stencil(weights, value, to_east, to_west, to_north, to_south):
    centre, w_east, w_west, w_north, w_south, w_below, w_above = weights
    return (
        (centre * value + (w_north * to_north + w_south * to_south))
        + (w_below * upward(value) + w_above * downward(value))
        + (w_east * to_east + w_west * to_west)
    )


def north_faces(get, r, tiles):
    return [
        face(get(V, r, k), get(K, r, k), get(M, r, k) * get(M, r + 1, k)) for k in range(tiles)
    ]


def row_weights(get, r, tiles, faces_north, faces_south, interface=None):
    sea = [get(M, r, k) for k in range(tiles)]
    faces = []
    for k in range(tiles):
        both = sea[k] * (east(sea[k], sea[k + 1]) if k + 1 < tiles else turn(sea[k], -1))
        faces.append(face(get(U, r, k), get(K, r, k), both))
    ends = faces[-1]
    if interface is not None:
        at_end = lanes() == LANES - 1
        faces[-1] = tuple(jnp.where(at_end, i, e) for i, e in zip(interface, ends))
        ends = tuple(jnp.where(at_end, turn(i, -1), e) for i, e in zip(interface, ends))
    weights = []
    for k in range(tiles):
        before = faces[k - 1] if k else ends
        faces_west = tuple(west(v, b) for v, b in zip(faces[k], before))
        faces_vertical = vertical(get(KZ, r, k), sea[k])
        weights.append(
            collected(sea[k], faces[k], faces_west, faces_north[k], faces_south[k], faces_vertical)
        )
    return weights


def pack_kernel(
    tracers, speed_east, speed_north, diff_horiz, diff_vert, sea,
    own, firsts, lasts, swap_even, swap_odd, loaded, loaded_sea, sems,
):
    tiles = own.shape[-1] // LANES
    even = is_even("zonal")
    lane = lanes()
    sources = (tracers.at[0], tracers.at[1], speed_east, speed_north, diff_horiz, diff_vert, sea)
    copies = [
        pltpu.make_async_copy(source, loaded_sea if f == M else loaded.at[f], sems.at[f])
        for f, source in enumerate(sources)
    ]
    for copy in copies:
        copy.start()

    for f in range(FIELDS):
        copies[f].wait()
        source = loaded_sea if f == M else loaded.at[f]
        first_cols = jnp.zeros((8, LANES), jnp.float32)
        last_cols = first_cols
        for r in range(ROWS):
            begin = OWN_LANE + COLS * r
            here = (lane >= begin) & (lane < begin + COLS)
            for k in range(tiles):
                value = source[pl.ds(8 * k + r, 8, stride=8 * tiles), :].astype(jnp.float32)
                own[f, r, :, pl.ds(k * LANES, LANES)] = value
                if k == 0:
                    first_cols = jnp.where(here, turn(value, begin), first_cols)
                if k == tiles - 1:
                    last_cols = jnp.where(here, turn(value, begin + COLS), last_cols)
        firsts[f] = first_cols
        lasts[f] = last_cols
        swap_even[f] = jnp.where(even, last_cols, first_cols)
        swap_odd[f] = jnp.where(even, first_cols, last_cols)


def border_kernel(own, swap_even, swap_odd, coef, state, kept):
    tiles = own.shape[-1] // LANES

    def put(item, k, value):
        for which, items in enumerate((TO_NORTH, TO_SOUTH)):
            if item in items:
                kept[which, items.index(item) * tiles + k] = value

    def get(f, r, k):
        return own[f, r, :, pl.ds(k * LANES, LANES)]

    for f in range(FIELDS):
        for r in range(ROWS):
            for k in range(tiles):
                put((0, f, r), k, get(f, r, k))

    faces = [north_faces(get, r, tiles) for r in range(0, ROWS - 1)]
    for r in range(1, ROWS - 1):
        weights = row_weights(get, r, tiles, faces[r], faces[r - 1])
        for k in range(tiles):
            cols = pl.ds(k * LANES, LANES)
            for i in range(7):
                coef[i, r, :, cols] = weights[k][i]

    for n in range(2):
        def read(t, r, k, n=n):
            return get(t, r, k) if n == 0 else state[t, r, :, pl.ds(k * LANES, LANES)]

        for r in range(1 + n, ROWS - 1 - n):
            for k in range(tiles):
                cols = pl.ds(k * LANES, LANES)
                weights = [coef[i, r, :, cols] for i in range(7)]
                for t in range(2):
                    value = read(t, r, k)
                    stepped = stencil(
                        weights,
                        value,
                        east(value, read(t, r, k + 1)) if k + 1 < tiles else turn(value, -1),
                        west(value, read(t, r, k - 1)) if k else turn(value, 1),
                        read(t, r + 1, k),
                        read(t, r - 1, k),
                    )
                    if n == 0:
                        state[t, r, :, cols] = stepped
                    put((n + 1, t, r), k, stepped)

    even = is_even("merid")

    @pl.when(even)
    def _():
        swap_even[...] = kept[0]
        swap_odd[...] = kept[1]

    @pl.when(jnp.logical_not(even))
    def _():
        swap_even[...] = kept[1]
        swap_odd[...] = kept[0]


def strips_kernel(firsts, lasts, zonal_even, zonal_odd, swap_even, swap_odd):
    lane = lanes()
    even = is_even("merid")
    even_zonal = is_even("zonal")
    for f in range(FIELDS):
        from_east = jnp.where(even_zonal, zonal_even[f], zonal_odd[f])
        from_west = jnp.where(even_zonal, zonal_odd[f], zonal_even[f])
        messages = []
        for pieces in (STRIPS_TO_NORTH, STRIPS_TO_SOUTH):
            message = jnp.zeros((8, LANES), jnp.float32)
            for strip, (begin, length, there, _) in zip(
                (firsts[f], lasts[f], from_east, from_west), pieces
            ):
                moved = turn(strip, there - begin)
                message = jnp.where((lane >= there) & (lane < there + length), moved, message)
            messages.append(message)
        swap_even[f] = jnp.where(even, messages[0], messages[1])
        swap_odd[f] = jnp.where(even, messages[1], messages[0])


def solve_kernel(
    own, rows_even, rows_odd, firsts, lasts, zonal_even, zonal_odd, strips_even, strips_odd,
    out, received, field, coef, state,
):
    tiles = own.shape[-1] // LANES
    lane = lanes()
    column = lax.rem(lane, COLS)
    at_first = column == 0
    at_last = column == COLS - 1

    even = is_even("merid")
    even_zonal = is_even("zonal")

    @pl.when(even)
    def _():
        received[0] = rows_odd[...]
        received[1] = rows_even[...]

    @pl.when(jnp.logical_not(even))
    def _():
        received[0] = rows_even[...]
        received[1] = rows_odd[...]

    def assembled(which, source):
        fields = []
        for f in range(FIELDS):
            value = source(f)
            strips_south = jnp.where(even, strips_odd[f], strips_even[f])
            strips_north = jnp.where(even, strips_even[f], strips_odd[f])
            for message, pieces in ((strips_south, STRIPS_TO_NORTH), (strips_north, STRIPS_TO_SOUTH)):
                _, length, there, begin = pieces[which]
                moved = turn(message, begin - there)
                value = jnp.where((lane >= begin) & (lane < begin + length), moved, value)
            fields.append(value)
        return fields

    own_first = assembled(0, lambda f: firsts[f])
    own_last = assembled(1, lambda f: lasts[f])
    east_first = assembled(2, lambda f: jnp.where(even_zonal, zonal_even[f], zonal_odd[f]))
    west_last = assembled(3, lambda f: jnp.where(even_zonal, zonal_odd[f], zonal_even[f]))

    def to_first(value):
        return turn(value, 1 - COLS)

    def to_last(value):
        return turn(value, COLS - 1)

    def strip_weights(left, right):
        both = left[M] * jnp.where(at_last, to_last(right[M]), turn(left[M], -1))
        left_faces = face(left[U], left[K], both)
        right_faces = face(right[U], right[K], right[M] * turn(right[M], -1))
        left_west = tuple(turn(v, 1) for v in left_faces)
        right_west = tuple(
            jnp.where(at_first, to_first(l), turn(v, 1)) for l, v in zip(left_faces, right_faces)
        )
        weights = []
        for strip, faces, faces_west in ((left, left_faces, left_west), (right, right_faces, right_west)):
            north = face(strip[V], strip[K], strip[M] * turn(strip[M], -COLS))
            south = tuple(turn(v, COLS) for v in north)
            weights.append(
                collected(strip[M], faces, faces_west, north, south, vertical(strip[KZ], strip[M]))
            )
        return weights[0], weights[1], left_faces

    w_west_last, w_own_first, west_face = strip_weights(west_last, own_first)
    w_own_last, w_east_first, east_face = strip_weights(own_last, east_first)

    def step_first(weights, value, ghost):
        return stencil(
            weights, value, turn(value, -1), jnp.where(at_first, ghost, turn(value, 1)),
            turn(value, -COLS), turn(value, COLS),
        )

    def step_last(weights, value, ghost):
        return stencil(
            weights, value, jnp.where(at_last, ghost, turn(value, -1)), turn(value, 1),
            turn(value, -COLS), turn(value, COLS),
        )

    def trace(value, ghost):
        return FACTOR_B * value - FACTOR_A * ghost

    def robin(told, value):
        return (told + FACTOR_A * value) * (1.0 / FACTOR_B)

    ghosts = []
    first_steps = []
    last_steps = []
    for t in range(2):
        ghost_first = to_first(west_last[t])
        ghost_last = to_last(east_first[t])
        a_first, a_last = own_first[t], own_last[t]
        b_first, b_last = east_first[t], west_last[t]
        c_first, c_last = own_first[t], own_last[t]
        ghosts_t = []
        steps_first, steps_last = [], []
        for n in range(STEPS):
            told_last = to_last(trace(a_first, ghost_first))
            told_first = to_first(trace(a_last, ghost_last))
            robin_last = robin(told_last, b_last)
            robin_first = robin(told_first, b_first)
            trace_last = trace(b_last, robin_last)
            trace_first = trace(b_first, robin_first)
            ghosts_t.append(
                jnp.where(at_last, trace_last, turn(trace_first, COLS - 2)) * (1.0 / FACTOR_B)
            )
            if n < STEPS - 1:
                a_first = step_first(w_own_first, a_first, ghost_first)
                a_last = step_last(w_own_last, a_last, ghost_last)
                b_first = step_first(w_east_first, b_first, robin_first)
                b_last = step_last(w_west_last, b_last, robin_last)
            if n < 2:
                c_first = step_first(w_own_first, c_first, robin(to_first(trace_last), c_first))
                c_last = step_last(w_own_last, c_last, robin(to_last(trace_first), c_last))
                steps_first.append(c_first)
                steps_last.append(c_last)
        ghosts.append(ghosts_t)
        first_steps.append(steps_first)
        last_steps.append(steps_last)

    def ends_of(value, r):
        return turn(value, -(COLS * (r + RIM) + COLS - 1))

    faces_at_ends = [
        jnp.where(at_last, w, turn(e, -1)) for w, e in zip(west_face, east_face)
    ]

    def cols(k):
        return pl.ds(k * LANES, LANES)

    for side, items, offset in ((0, TO_NORTH, -ROWS), (1, TO_SOUTH, ROWS)):
        for i, (n, f, r) in enumerate(items):
            r = r + offset
            for k in range(tiles):
                value = received[side, i * tiles + k]
                if n and k == 0:
                    fixed = turn(first_steps[f][n - 1], -COLS * (r + RIM))
                    value = jnp.where(lane < n, fixed, value)
                if n and k == tiles - 1:
                    fixed = turn(last_steps[f][n - 1], -COLS * (r + RIM + 1))
                    value = jnp.where(lane >= LANES - n, fixed, value)
                if f < 2:
                    state[n % 2, f, r + BORDER, :, cols(k)] = value
                else:
                    field[f, r + BORDER, :, cols(k)] = value

    def get(f, r, k):
        if 0 <= r < ROWS:
            return own[f, r, :, cols(k)]
        return field[f, r + BORDER, :, cols(k)]

    def read(n, t, r, k):
        if n == 0 and 0 <= r < ROWS:
            return own[t, r, :, cols(k)]
        return state[n % 2, t, r + BORDER, :, cols(k)]

    reach = BORDER - 1
    faces_south = north_faces(get, -reach - 1, tiles)
    for r in range(-reach, ROWS + reach):
        faces_north = north_faces(get, r, tiles)
        interface = tuple(ends_of(v, r) for v in faces_at_ends)
        weights = row_weights(get, r, tiles, faces_north, faces_south, interface)
        faces_south = faces_north
        for k in range(tiles):
            for i in range(7):
                coef[i, r + BORDER, :, cols(k)] = weights[k][i]

    for n in range(STEPS):
        more = min(n + 1, STEPS - 1 - n)
        for r in range(-more, ROWS + more):
            ends = [ends_of(ghosts[t][n], r) for t in range(2)]
            for k in range(tiles):
                weights = [coef[i, r + BORDER, :, cols(k)] for i in range(7)]
                for t in range(2):
                    value = read(n, t, r, k)
                    if k == 0 or k == tiles - 1:
                        ghost = ends[t] + (FACTOR_A / FACTOR_B) * value
                    if k == 0:
                        to_west = jnp.where(lane == 0, ghost, turn(value, 1))
                    else:
                        to_west = west(value, read(n, t, r, k - 1))
                    if k == tiles - 1:
                        to_east = jnp.where(lane == LANES - 1, ghost, turn(value, -1))
                    else:
                        to_east = east(value, read(n, t, r, k + 1))
                    stepped = stencil(
                        weights, value, to_east, to_west, read(n, t, r + 1, k), read(n, t, r - 1, k)
                    )
                    if n == STEPS - 1:
                        out[t, pl.ds(8 * k + r, 8, stride=8 * tiles), :] = stepped
                    else:
                        state[(n + 1) % 2, t, r + BORDER, :, cols(k)] = stepped


def granted(mib=16):
    return pltpu.CompilerParams(vmem_limit_bytes=mib * 1024 * 1024)


def long_work():
    return pl.CostEstimate(flops=100_000_000_000, bytes_accessed=1_000_000_000, transcendentals=0)


def in_vmem(count):
    return [pl.BlockSpec(memory_space=pltpu.VMEM)] * count


def in_tiles(array):
    lead = array.shape[:-2]
    tiled = array.reshape(lead + (8, -1, LANES))
    return jnp.swapaxes(tiled, -3, -2).reshape(lead[:-1] + (-1, LANES))


def from_tiles(array, shape):
    tiled = array.reshape(shape[:-2] + (-1, 8, LANES))
    return jnp.swapaxes(tiled, -3, -2).reshape(shape)


def pack(*arrays):
    f32 = jnp.float32
    width = arrays[1].size // 64
    return pl.pallas_call(
        pack_kernel,
        out_shape=(
            jax.ShapeDtypeStruct((FIELDS, ROWS, 8, width), f32),
        )
        + (jax.ShapeDtypeStruct((FIELDS, 8, LANES), f32),) * 4,
        in_specs=[pl.BlockSpec(memory_space=pltpu.HBM)] * 6,
        out_specs=tuple(in_vmem(5)),
        scratch_shapes=[
            pltpu.VMEM((M,) + arrays[1].shape, f32),
            pltpu.VMEM(arrays[5].shape, arrays[5].dtype),
            pltpu.SemaphoreType.DMA((FIELDS,)),
        ],
        compiler_params=granted(),
        name="pack",
    )(*arrays)


def border(own):
    f32 = jnp.float32
    width = own.shape[-1]
    message = (len(TO_NORTH) * width // LANES, 8, LANES)
    return pl.pallas_call(
        border_kernel,
        out_shape=(jax.ShapeDtypeStruct(message, f32),) * 2,
        in_specs=in_vmem(1),
        out_specs=tuple(in_vmem(2)),
        scratch_shapes=[
            pltpu.VMEM((7, ROWS, 8, width), f32),
            pltpu.VMEM((2, ROWS, 8, width), f32),
            pltpu.VMEM((2,) + message, f32),
        ],
        compiler_params=granted(),
        cost_estimate=long_work(),
        name="border",
    )(own)


def exchange_strips(*strips):
    shape = jax.ShapeDtypeStruct((FIELDS, 8, LANES), jnp.float32)
    return pl.pallas_call(
        strips_kernel,
        out_shape=(shape, shape),
        in_specs=in_vmem(4),
        out_specs=tuple(in_vmem(2)),
        compiler_params=granted(),
        cost_estimate=long_work(),
        name="strips",
    )(*strips)


def solve(own, *others):
    f32 = jnp.float32
    width = own.shape[-1]
    rows = ROWS + 2 * BORDER
    return pl.pallas_call(
        solve_kernel,
        out_shape=jax.ShapeDtypeStruct((2, width // LANES * 64, LANES), f32),
        in_specs=in_vmem(9),
        out_specs=in_vmem(1)[0],
        scratch_shapes=[
            pltpu.VMEM((2,) + others[0].shape, f32),
            pltpu.VMEM((FIELDS, rows, 8, width), f32),
            pltpu.VMEM((7, rows, 8, width), f32),
            pltpu.VMEM((2, 2, rows, 8, width), f32),
        ],
        compiler_params=granted(),
        name="solve",
    )(own, *others)


def swapped(axis, arrays, periodic):
    count = lax.axis_size(axis)
    received = []
    for start, array in enumerate(arrays):
        pairs = [(i, (i + 1) % count) for i in range(start, count, 2) if periodic or i + 1 < count]
        received.append(lax.ppermute(array, axis, pairs + [(b, a) for a, b in pairs]))
    return received


def shards(tracers, speed_east, speed_north, diff_horiz, diff_vert, sea_mask):
    arrays = (tracers, speed_east, speed_north, diff_horiz, diff_vert, sea_mask)
    own, firsts, lasts, *zonal = pack(
        *[pltpu.with_memory_space_constraint(in_tiles(a), pltpu.HBM) for a in arrays]
    )
    zonal = swapped("zonal", zonal, True)
    rows = swapped("merid", border(own), False)
    strips = swapped("merid", exchange_strips(firsts, lasts, *zonal), False)
    result = solve(own, *rows, firsts, lasts, *zonal, *strips)
    return from_tiles(result, tracers.shape)


def solution(mesh):
    row = P(None, "merid", "zonal")
    whole = P(None, None, "merid", "zonal")
    return jax.shard_map(
        shards, mesh=mesh, in_specs=(whole, row, row, row, row, row), out_specs=whole, check_vma=False
    )
```

```python
import jax
import jax.numpy as jnp
from jax import lax
from jax.experimental import pallas as pl
from jax.experimental.pallas import tpu as pltpu
from jax.sharding import PartitionSpec as P

STEPS = 6
LANES = 128
ROWS = 8

ROBIN_WEIGHT = 0.5
FACTOR_A = 1.0 - ROBIN_WEIGHT / 2.0
FACTOR_B = 1.0 + ROBIN_WEIGHT / 2.0

U, V, K, KZ, M = 2, 3, 4, 5, 6
FIELDS = 7

PART, FACE = 3, 4
TO_SOUTH = (
    [(n, t, n) for t in (0, 1) for n in (0, 1, 2)]
    + [(PART, t, n) for t in (0, 1) for n in (0, 1, 2)]
    + [(0, f, r) for f in (U, V, K, KZ) for r in (0, 1)]
    + [(0, M, r) for r in (0, 1, 2)]
)
TO_NORTH = (
    [(n, t, 7 - n) for t in (0, 1) for n in (0, 1, 2)]
    + [(PART, t, 7 - n) for t in (0, 1) for n in (0, 1, 2)]
    + [(0, f, r) for f in (U, V, K, KZ, M) for r in (6, 7)]
    + [(FACE, i, 5) for i in (0, 1)]
)
UNITS = max(len(TO_SOUTH), len(TO_NORTH))
BORDER = 3

COLS = 6
RIM = 6
OWN_LANE = COLS * RIM

STRIPS_TO_SOUTH = ((36, 33, 0, 84), (36, 36, 33, 84), (36, 25, 69, 84), (36, 30, 94, 84))
STRIPS_TO_NORTH = ((48, 36, 0, 0), (51, 33, 36, 3), (54, 30, 69, 6), (59, 25, 99, 11))


def lanes():
    return lax.broadcasted_iota(jnp.int32, (8, LANES), 1)


def is_even(axis):
    return lax.rem(lax.axis_index(axis), 2) == 0


def turn(value, shift):
    shift = shift % LANES
    return pltpu.roll(value, shift, 1) if shift else value


def upward(value):
    return pltpu.roll(value, 7, 0)


def downward(value):
    return pltpu.roll(value, 1, 0)


def west(value, beside):
    return turn(jnp.where(lanes() == LANES - 1, beside, value), 1)


def east(value, beside):
    return turn(jnp.where(lanes() == 0, beside, value), -1)


def face(speed, diff, both):
    return (jnp.maximum(speed, 0.0) + diff) * both, (jnp.minimum(speed, 0.0) - diff) * both


def vertical(diff, sea):
    level = lax.broadcasted_iota(jnp.int32, (8, LANES), 0)
    below = diff * sea * jnp.where(level == 7, 0.0, upward(sea))
    return below, downward(below)


def collected(sea, faces_east, faces_west, faces_north, faces_south, faces_vertical):
    here, there = faces_east
    here_west, there_west = faces_west
    north_here, north_there = faces_north
    south_here, south_there = faces_south
    below, above = faces_vertical
    centre = sea - ((here - there_west) + (north_here - south_there) + (below + above))
    return centre, -there, here_west, -north_there, south_here, below, above


def stencil(weights, value, to_east, to_west, to_north, to_south):
    centre, w_east, w_west, w_north, w_south, w_below, w_above = weights
    return (
        (centre * value + (w_north * to_north + w_south * to_south))
        + (w_below * upward(value) + w_above * downward(value))
        + (w_east * to_east + w_west * to_west)
    )


def north_faces(get, r, tiles):
    return [
        face(get(V, r, k), get(K, r, k), get(M, r, k) * get(M, r + 1, k)) for k in range(tiles)
    ]


def row_weights(get, r, tiles, faces_north, faces_south, interface=None):
    sea = [get(M, r, k) for k in range(tiles)]
    faces = []
    for k in range(tiles):
        both = sea[k] * (east(sea[k], sea[k + 1]) if k + 1 < tiles else turn(sea[k], -1))
        faces.append(face(get(U, r, k), get(K, r, k), both))
    ends = faces[-1]
    if interface is not None:
        at_end = lanes() == LANES - 1
        faces[-1] = tuple(jnp.where(at_end, i, e) for i, e in zip(interface, ends))
        ends = tuple(jnp.where(at_end, turn(i, -1), e) for i, e in zip(interface, ends))
    weights = []
    for k in range(tiles):
        before = faces[k - 1] if k else ends
        faces_west = tuple(west(v, b) for v, b in zip(faces[k], before))
        faces_vertical = vertical(get(KZ, r, k), sea[k])
        weights.append(
            collected(sea[k], faces[k], faces_west, faces_north[k], faces_south[k], faces_vertical)
        )
    return weights


def pack_kernel(
    tracers, speed_east, speed_north, diff_horiz, diff_vert, sea,
    own, firsts, lasts, swap_even, swap_odd, loaded, loaded_sea, sems,
):
    tiles = own.shape[-1] // LANES
    even = is_even("zonal")
    lane = lanes()
    sources = (tracers.at[0], tracers.at[1], speed_east, speed_north, diff_horiz, diff_vert, sea)
    copies = [
        pltpu.make_async_copy(source, loaded_sea if f == M else loaded.at[f], sems.at[f])
        for f, source in enumerate(sources)
    ]
    for copy in copies:
        copy.start()

    for f in range(FIELDS):
        copies[f].wait()
        source = loaded_sea if f == M else loaded.at[f]
        first_cols = jnp.zeros((8, LANES), jnp.float32)
        last_cols = first_cols
        for r in range(ROWS):
            begin = OWN_LANE + COLS * r
            here = (lane >= begin) & (lane < begin + COLS)
            for k in range(tiles):
                value = source[pl.ds(8 * k + r, 8, stride=8 * tiles), :].astype(jnp.float32)
                own[f, r, :, pl.ds(k * LANES, LANES)] = value
                if k == 0:
                    first_cols = jnp.where(here, turn(value, begin), first_cols)
                if k == tiles - 1:
                    last_cols = jnp.where(here, turn(value, begin + COLS), last_cols)
        firsts[f] = first_cols
        lasts[f] = last_cols
        swap_even[f] = jnp.where(even, last_cols, first_cols)
        swap_odd[f] = jnp.where(even, first_cols, last_cols)


def border_kernel(own, swap_even, swap_odd, coef, state, kept):
    tiles = own.shape[-1] // LANES

    def put(item, k, value):
        for which, items in enumerate((TO_NORTH, TO_SOUTH)):
            if item in items:
                kept[which, items.index(item) * tiles + k] = value

    def get(f, r, k):
        return own[f, r, :, pl.ds(k * LANES, LANES)]

    for f in range(FIELDS):
        for r in range(ROWS):
            for k in range(tiles):
                put((0, f, r), k, get(f, r, k))

    closed = [(jnp.zeros((8, LANES), jnp.float32),) * 2] * tiles
    faces_south = closed
    for r in range(ROWS):
        faces_north = north_faces(get, r, tiles) if r + 1 < ROWS else closed
        weights = row_weights(get, r, tiles, faces_north, faces_south)
        faces_south = faces_north
        for k in range(tiles):
            for i in range(7):
                coef[i, r, :, pl.ds(k * LANES, LANES)] = weights[k][i]
            for i in range(2):
                put((FACE, i, r), k, faces_north[k][i])

    for n in range(3):
        def read(t, r, k, n=n):
            return get(t, r, k) if n == 0 else state[n - 1, t, r, :, pl.ds(k * LANES, LANES)]

        for r in range(n, ROWS - n):
            if n == 2 and r not in (n, ROWS - 1 - n):
                continue
            for k in range(tiles):
                cols = pl.ds(k * LANES, LANES)
                weights = [coef[i, r, :, cols] for i in range(7)]
                for t in range(2):
                    value = read(t, r, k)
                    to_north = read(t, r + 1, k) if r + 1 < ROWS - n else 0.0
                    to_south = read(t, r - 1, k) if r > n else 0.0
                    stepped = stencil(
                        weights,
                        value,
                        east(value, read(t, r, k + 1)) if k + 1 < tiles else turn(value, -1),
                        west(value, read(t, r, k - 1)) if k else turn(value, 1),
                        to_north,
                        to_south,
                    )
                    if r == n:
                        if n:
                            stepped = stepped + coef[3, r - 1, :, cols] * value
                        put((PART, t, r), k, stepped)
                    elif r == ROWS - 1 - n:
                        if n:
                            stepped = stepped + coef[4, r + 1, :, cols] * value
                        put((PART, t, r), k, stepped)
                    else:
                        state[n, t, r, :, cols] = stepped
                        put((n + 1, t, r), k, stepped)

    even = is_even("merid")

    @pl.when(even)
    def _():
        swap_even[...] = kept[0]
        swap_odd[...] = kept[1]

    @pl.when(jnp.logical_not(even))
    def _():
        swap_even[...] = kept[1]
        swap_odd[...] = kept[0]


def strips_kernel(firsts, lasts, zonal_even, zonal_odd, swap_even, swap_odd):
    lane = lanes()
    even = is_even("merid")
    even_zonal = is_even("zonal")
    for f in range(FIELDS):
        from_east = jnp.where(even_zonal, zonal_even[f], zonal_odd[f])
        from_west = jnp.where(even_zonal, zonal_odd[f], zonal_even[f])
        messages = []
        for pieces in (STRIPS_TO_NORTH, STRIPS_TO_SOUTH):
            message = jnp.zeros((8, LANES), jnp.float32)
            for strip, (begin, length, there, _) in zip(
                (firsts[f], lasts[f], from_east, from_west), pieces
            ):
                moved = turn(strip, there - begin)
                message = jnp.where((lane >= there) & (lane < there + length), moved, message)
            messages.append(message)
        swap_even[f] = jnp.where(even, messages[0], messages[1])
        swap_odd[f] = jnp.where(even, messages[1], messages[0])


def solve_kernel(
    own, rows_even, rows_odd, firsts, lasts, zonal_even, zonal_odd, strips_even, strips_odd,
    out, field, coef, state, part,
):
    tiles = own.shape[-1] // LANES
    lane = lanes()
    column = lax.rem(lane, COLS)
    at_first = column == 0
    at_last = column == COLS - 1

    even = is_even("merid")
    even_zonal = is_even("zonal")

    def cols(k):
        return pl.ds(k * LANES, LANES)

    def unpack(source, items, offset):
        for i, (n, f, r) in enumerate(items):
            e = r + offset + BORDER
            for k in range(tiles):
                value = source[i * tiles + k]
                if n == FACE:
                    coef[3 + f, e, :, cols(k)] = value
                elif n == PART:
                    part[f, e, :, cols(k)] = value
                elif f < 2:
                    state[n % 2, f, e, :, cols(k)] = value
                else:
                    field[f, e, :, cols(k)] = value

    @pl.when(even)
    def _():
        unpack(rows_odd, TO_NORTH, -ROWS)
        unpack(rows_even, TO_SOUTH, ROWS)

    @pl.when(jnp.logical_not(even))
    def _():
        unpack(rows_even, TO_NORTH, -ROWS)
        unpack(rows_odd, TO_SOUTH, ROWS)

    def assembled(which, source):
        fields = []
        for f in range(FIELDS):
            value = source(f)
            strips_south = jnp.where(even, strips_odd[f], strips_even[f])
            strips_north = jnp.where(even, strips_even[f], strips_odd[f])
            for message, pieces in ((strips_south, STRIPS_TO_NORTH), (strips_north, STRIPS_TO_SOUTH)):
                _, length, there, begin = pieces[which]
                moved = turn(message, begin - there)
                value = jnp.where((lane >= begin) & (lane < begin + length), moved, value)
            fields.append(value)
        return fields

    own_first = assembled(0, lambda f: firsts[f])
    own_last = assembled(1, lambda f: lasts[f])
    east_first = assembled(2, lambda f: jnp.where(even_zonal, zonal_even[f], zonal_odd[f]))
    west_last = assembled(3, lambda f: jnp.where(even_zonal, zonal_odd[f], zonal_even[f]))

    def to_first(value):
        return turn(value, 1 - COLS)

    def to_last(value):
        return turn(value, COLS - 1)

    def strip_weights(left, right):
        both = left[M] * jnp.where(at_last, to_last(right[M]), turn(left[M], -1))
        left_faces = face(left[U], left[K], both)
        right_faces = face(right[U], right[K], right[M] * turn(right[M], -1))
        left_west = tuple(turn(v, 1) for v in left_faces)
        right_west = tuple(
            jnp.where(at_first, to_first(l), turn(v, 1)) for l, v in zip(left_faces, right_faces)
        )
        weights = []
        for strip, faces, faces_west in ((left, left_faces, left_west), (right, right_faces, right_west)):
            north = face(strip[V], strip[K], strip[M] * turn(strip[M], -COLS))
            south = tuple(turn(v, COLS) for v in north)
            weights.append(
                collected(strip[M], faces, faces_west, north, south, vertical(strip[KZ], strip[M]))
            )
        return weights[0], weights[1], left_faces

    w_west_last, w_own_first, west_face = strip_weights(west_last, own_first)
    w_own_last, w_east_first, east_face = strip_weights(own_last, east_first)

    def step_first(weights, value, ghost):
        return stencil(
            weights, value, turn(value, -1), jnp.where(at_first, ghost, turn(value, 1)),
            turn(value, -COLS), turn(value, COLS),
        )

    def step_last(weights, value, ghost):
        return stencil(
            weights, value, jnp.where(at_last, ghost, turn(value, -1)), turn(value, 1),
            turn(value, -COLS), turn(value, COLS),
        )

    def trace(value, ghost):
        return FACTOR_B * value - FACTOR_A * ghost

    def robin(told, value):
        return (told + FACTOR_A * value) * (1.0 / FACTOR_B)

    ghosts = []
    first_steps = []
    last_steps = []
    for t in range(2):
        ghost_first = to_first(west_last[t])
        ghost_last = to_last(east_first[t])
        a_first, a_last = own_first[t], own_last[t]
        b_first, b_last = east_first[t], west_last[t]
        c_first, c_last = own_first[t], own_last[t]
        ghosts_t = []
        steps_first, steps_last = [], []
        for n in range(STEPS):
            told_last = to_last(trace(a_first, ghost_first))
            told_first = to_first(trace(a_last, ghost_last))
            robin_last = robin(told_last, b_last)
            robin_first = robin(told_first, b_first)
            trace_last = trace(b_last, robin_last)
            trace_first = trace(b_first, robin_first)
            ghosts_t.append(
                jnp.where(at_last, trace_last, turn(trace_first, COLS - 2)) * (1.0 / FACTOR_B)
            )
            if n < STEPS - 1:
                a_first = step_first(w_own_first, a_first, ghost_first)
                a_last = step_last(w_own_last, a_last, ghost_last)
                b_first = step_first(w_east_first, b_first, robin_first)
                b_last = step_last(w_west_last, b_last, robin_last)
            if n < 3:
                c_first = step_first(w_own_first, c_first, robin(to_first(trace_last), c_first))
                c_last = step_last(w_own_last, c_last, robin(to_last(trace_first), c_last))
                steps_first.append(c_first)
                steps_last.append(c_last)
        ghosts.append(ghosts_t)
        first_steps.append(steps_first)
        last_steps.append(steps_last)

    def ends_of(value, r):
        return turn(value, -(COLS * (r + RIM) + COLS - 1))

    faces_at_ends = [
        jnp.where(at_last, w, turn(e, -1)) for w, e in zip(west_face, east_face)
    ]

    def fixed(value, n, t, r, k):
        if n and k == 0:
            exact = turn(first_steps[t][n - 1], -COLS * (r + RIM))
            value = jnp.where(lane < n, exact, value)
        if n and k == tiles - 1:
            exact = turn(last_steps[t][n - 1], -COLS * (r + RIM + 1))
            value = jnp.where(lane >= LANES - n, exact, value)
        return value

    for n in (1, 2):
        for t in range(2):
            for r in (-1 - n, ROWS + n):
                for k in (0, tiles - 1):
                    value = state[n % 2, t, r + BORDER, :, cols(k)]
                    state[n % 2, t, r + BORDER, :, cols(k)] = fixed(value, n, t, r, k)

    def get(f, r, k):
        if 0 <= r < ROWS:
            return own[f, r, :, cols(k)]
        return field[f, r + BORDER, :, cols(k)]

    def read(n, t, r, k):
        if n == 0 and 0 <= r < ROWS:
            return own[t, r, :, cols(k)]
        return state[n % 2, t, r + BORDER, :, cols(k)]

    faces_south = []
    for k in range(tiles):
        here, there = (coef[i, 0, :, cols(k)] for i in (3, 4))
        faces_south.append((here, there))
        coef[3, 0, :, cols(k)] = -there
    reach = BORDER - 1
    for r in range(-reach, ROWS + reach):
        faces_north = north_faces(get, r, tiles)
        interface = tuple(ends_of(v, r) for v in faces_at_ends)
        weights = row_weights(get, r, tiles, faces_north, faces_south, interface)
        faces_south = faces_north
        for k in range(tiles):
            for i in range(7):
                coef[i, r + BORDER, :, cols(k)] = weights[k][i]
    for k in range(tiles):
        coef[4, ROWS + reach + BORDER, :, cols(k)] = faces_south[k][0]

    for n in range(STEPS):
        if n < BORDER:
            for t in range(2):
                for k in range(tiles):
                    r = -1 - n
                    e = r + BORDER
                    stepped = (
                        part[t, e, :, cols(k)]
                        + coef[3, e, :, cols(k)] * read(n, t, r + 1, k)
                        - coef[4, e + 1, :, cols(k)] * read(n, t, r, k)
                    )
                    state[(n + 1) % 2, t, e, :, cols(k)] = fixed(stepped, n + 1, t, r, k)
                    r = ROWS + n
                    e = r + BORDER
                    stepped = (
                        part[t, e, :, cols(k)]
                        + coef[4, e, :, cols(k)] * read(n, t, r - 1, k)
                        - coef[3, e - 1, :, cols(k)] * read(n, t, r, k)
                    )
                    state[(n + 1) % 2, t, e, :, cols(k)] = fixed(stepped, n + 1, t, r, k)
        more = min(n, STEPS - 1 - n)
        for r in range(-more, ROWS + more):
            ends = [ends_of(ghosts[t][n], r) for t in range(2)]
            for k in range(tiles):
                weights = [coef[i, r + BORDER, :, cols(k)] for i in range(7)]
                for t in range(2):
                    value = read(n, t, r, k)
                    if k == 0 or k == tiles - 1:
                        ghost = ends[t] + (FACTOR_A / FACTOR_B) * value
                    if k == 0:
                        to_west = jnp.where(lane == 0, ghost, turn(value, 1))
                    else:
                        to_west = west(value, read(n, t, r, k - 1))
                    if k == tiles - 1:
                        to_east = jnp.where(lane == LANES - 1, ghost, turn(value, -1))
                    else:
                        to_east = east(value, read(n, t, r, k + 1))
                    stepped = stencil(
                        weights, value, to_east, to_west, read(n, t, r + 1, k), read(n, t, r - 1, k)
                    )
                    if n == STEPS - 1:
                        out[t, pl.ds(8 * k + r, 8, stride=8 * tiles), :] = stepped
                    else:
                        state[(n + 1) % 2, t, r + BORDER, :, cols(k)] = stepped


def granted(mib=16):
    return pltpu.CompilerParams(vmem_limit_bytes=mib * 1024 * 1024)


def long_work():
    return pl.CostEstimate(flops=100_000_000_000, bytes_accessed=1_000_000_000, transcendentals=0)


def in_vmem(count):
    return [pl.BlockSpec(memory_space=pltpu.VMEM)] * count


def in_tiles(array):
    lead = array.shape[:-2]
    tiled = array.reshape(lead + (8, -1, LANES))
    return jnp.swapaxes(tiled, -3, -2).reshape(lead[:-1] + (-1, LANES))


def from_tiles(array, shape):
    tiled = array.reshape(shape[:-2] + (-1, 8, LANES))
    return jnp.swapaxes(tiled, -3, -2).reshape(shape)


def pack(*arrays):
    f32 = jnp.float32
    width = arrays[1].size // 64
    return pl.pallas_call(
        pack_kernel,
        out_shape=(
            jax.ShapeDtypeStruct((FIELDS, ROWS, 8, width), f32),
        )
        + (jax.ShapeDtypeStruct((FIELDS, 8, LANES), f32),) * 4,
        in_specs=[pl.BlockSpec(memory_space=pltpu.HBM)] * 6,
        out_specs=tuple(in_vmem(5)),
        scratch_shapes=[
            pltpu.VMEM((M,) + arrays[1].shape, f32),
            pltpu.VMEM(arrays[5].shape, arrays[5].dtype),
            pltpu.SemaphoreType.DMA((FIELDS,)),
        ],
        compiler_params=granted(),
        name="pack",
    )(*arrays)


def border(own):
    f32 = jnp.float32
    width = own.shape[-1]
    message = (UNITS * width // LANES, 8, LANES)
    return pl.pallas_call(
        border_kernel,
        out_shape=(jax.ShapeDtypeStruct(message, f32),) * 2,
        in_specs=in_vmem(1),
        out_specs=tuple(in_vmem(2)),
        scratch_shapes=[
            pltpu.VMEM((7, ROWS, 8, width), f32),
            pltpu.VMEM((2, 2, ROWS, 8, width), f32),
            pltpu.VMEM((2,) + message, f32),
        ],
        compiler_params=granted(),
        cost_estimate=long_work(),
        name="border",
    )(own)


def exchange_strips(*strips):
    shape = jax.ShapeDtypeStruct((FIELDS, 8, LANES), jnp.float32)
    return pl.pallas_call(
        strips_kernel,
        out_shape=(shape, shape),
        in_specs=in_vmem(4),
        out_specs=tuple(in_vmem(2)),
        compiler_params=granted(),
        cost_estimate=long_work(),
        name="strips",
    )(*strips)


def solve(own, *others):
    f32 = jnp.float32
    width = own.shape[-1]
    rows = ROWS + 2 * BORDER
    return pl.pallas_call(
        solve_kernel,
        out_shape=jax.ShapeDtypeStruct((2, width // LANES * 64, LANES), f32),
        in_specs=in_vmem(9),
        out_specs=in_vmem(1)[0],
        scratch_shapes=[
            pltpu.VMEM((FIELDS, rows, 8, width), f32),
            pltpu.VMEM((7, rows, 8, width), f32),
            pltpu.VMEM((2, 2, rows, 8, width), f32),
            pltpu.VMEM((2, rows, 8, width), f32),
        ],
        compiler_params=granted(),
        name="solve",
    )(own, *others)


def swapped(axis, arrays, periodic):
    count = lax.axis_size(axis)
    received = []
    for start, array in enumerate(arrays):
        pairs = [(i, (i + 1) % count) for i in range(start, count, 2) if periodic or i + 1 < count]
        received.append(lax.ppermute(array, axis, pairs + [(b, a) for a, b in pairs]))
    return received


def shards(tracers, speed_east, speed_north, diff_horiz, diff_vert, sea_mask):
    arrays = (tracers, speed_east, speed_north, diff_horiz, diff_vert, sea_mask)
    own, firsts, lasts, *zonal = pack(
        *[pltpu.with_memory_space_constraint(in_tiles(a), pltpu.HBM) for a in arrays]
    )
    zonal = swapped("zonal", zonal, True)
    rows = swapped("merid", border(own), False)
    strips = swapped("merid", exchange_strips(firsts, lasts, *zonal), False)
    result = solve(own, *rows, firsts, lasts, *zonal, *strips)
    return from_tiles(result, tracers.shape)


def solution(mesh):
    row = P(None, "merid", "zonal")
    whole = P(None, None, "merid", "zonal")
    return jax.shard_map(
        shards, mesh=mesh, in_specs=(whole, row, row, row, row, row), out_specs=whole, check_vma=False
    )
```

```python
import jax
import jax.numpy as jnp
from jax import lax
from jax.experimental import pallas as pl
from jax.experimental.pallas import tpu as pltpu
from jax.sharding import PartitionSpec as P

STEPS = 6
LANES = 128
ROWS = 8

ROBIN_WEIGHT = 0.5
FACTOR_A = 1.0 - ROBIN_WEIGHT / 2.0
FACTOR_B = 1.0 + ROBIN_WEIGHT / 2.0

U, V, K, KZ, M = 2, 3, 4, 5, 6
FIELDS = 7

PART, FACE = 3, 4
TO_SOUTH = (
    [(n, t, n) for t in (0, 1) for n in (0, 1, 2)]
    + [(PART, t, n) for t in (0, 1) for n in (0, 1, 2)]
    + [(0, f, r) for f in (U, V, K, KZ) for r in (0, 1)]
    + [(0, M, r) for r in (0, 1, 2)]
)
TO_NORTH = (
    [(n, t, 7 - n) for t in (0, 1) for n in (0, 1, 2)]
    + [(PART, t, 7 - n) for t in (0, 1) for n in (0, 1, 2)]
    + [(0, f, r) for f in (U, V, K, KZ, M) for r in (6, 7)]
    + [(FACE, i, 5) for i in (0, 1)]
)
UNITS = max(len(TO_SOUTH), len(TO_NORTH))
BORDER = 3
BORDER_GROUP = 4
GROUP = 6

COLS = 6
RIM = 6
OWN_LANE = COLS * RIM

STRIPS_TO_SOUTH = ((36, 33, 0, 84), (36, 36, 33, 84), (36, 25, 69, 84), (36, 30, 94, 84))
STRIPS_TO_NORTH = ((48, 36, 0, 0), (51, 33, 36, 3), (54, 30, 69, 6), (59, 25, 99, 11))


def lanes():
    return lax.broadcasted_iota(jnp.int32, (8, LANES), 1)


def is_even(axis):
    return lax.rem(lax.axis_index(axis), 2) == 0


def turn(value, shift):
    shift = shift % LANES
    return pltpu.roll(value, shift, 1) if shift else value


def upward(value):
    return pltpu.roll(value, 7, 0)


def downward(value):
    return pltpu.roll(value, 1, 0)


def west(value, beside):
    return turn(jnp.where(lanes() == LANES - 1, beside, value), 1)


def east(value, beside):
    return turn(jnp.where(lanes() == 0, beside, value), -1)


def face(speed, diff, both):
    return (jnp.maximum(speed, 0.0) + diff) * both, (jnp.minimum(speed, 0.0) - diff) * both


def vertical(diff, sea):
    level = lax.broadcasted_iota(jnp.int32, (8, LANES), 0)
    below = diff * sea * jnp.where(level == 7, 0.0, upward(sea))
    return below, downward(below)


def collected(sea, faces_east, faces_west, faces_north, faces_south, faces_vertical):
    here, there = faces_east
    here_west, there_west = faces_west
    north_here, north_there = faces_north
    south_here, south_there = faces_south
    below, above = faces_vertical
    centre = sea - ((here - there_west) + (north_here - south_there) + (below + above))
    return centre, -there, here_west, -north_there, south_here, below, above


def weighted(weights, values):
    centre, w_east, w_west, w_north, w_south, w_below, w_above = weights
    value, to_east, to_west, to_north, to_south, below, above = values
    return (
        (centre * value + (w_north * to_north + w_south * to_south))
        + (w_below * below + w_above * above)
        + (w_east * to_east + w_west * to_west)
    )


def stencil(weights, value, to_east, to_west, to_north, to_south):
    values = (value, to_east, to_west, to_north, to_south, upward(value), downward(value))
    return weighted(weights, values)


def north_faces(get, r, tiles):
    return [
        face(get(V, r, k), get(K, r, k), get(M, r, k) * get(M, r + 1, k)) for k in range(tiles)
    ]


def weights_of(get, rows, tiles, faces_north, faces_south, interfaces=None):
    lane = lanes()
    cells = [(r, k) for r in rows for k in range(tiles)]
    sea = {(r, k): get(M, r, k) for r, k in cells}
    beside = {
        (r, k): east(sea[r, k], sea[r, k + 1]) if k + 1 < tiles else turn(sea[r, k], -1) for r, k in cells
    }
    beneath = {c: upward(sea[c]) for c in cells}
    bottom = lax.broadcasted_iota(jnp.int32, (8, LANES), 0) == 7
    faces, below = {}, {}
    for c in cells:
        faces[c] = face(get(U, *c), get(K, *c), sea[c] * beside[c])
        below[c] = get(KZ, *c) * sea[c] * jnp.where(bottom, 0.0, beneath[c])
    before = {}
    for i, r in enumerate(rows):
        ends = faces[r, tiles - 1]
        if interfaces is not None:
            at_end = lane == LANES - 1
            faces[r, tiles - 1] = tuple(
                jnp.where(at_end, turned, end) for turned, end in zip(interfaces[i], ends)
            )
            ends = tuple(turn(v, -1) for v in interfaces[i])
        before[r] = ends
    above = {c: downward(below[c]) for c in cells}
    faces_west = {}
    for r, k in cells:
        others = faces[r, k - 1] if k else before[r]
        faces_west[r, k] = tuple(west(v, b) for v, b in zip(faces[r, k], others))
    return [
        [
            collected(
                sea[r, k], faces[r, k], faces_west[r, k], faces_north[i][k], faces_south[i][k],
                (below[r, k], above[r, k]),
            )
            for k in range(tiles)
        ]
        for i, r in enumerate(rows)
    ]


def pack_kernel(
    tracers, speed_east, speed_north, diff_horiz, diff_vert, sea,
    own, firsts, lasts, swap_even, swap_odd, loaded, loaded_sea, sems,
):
    tiles = own.shape[-1] // LANES
    even = is_even("zonal")
    lane = lanes()
    sources = (tracers.at[0], tracers.at[1], speed_east, speed_north, diff_horiz, diff_vert, sea)
    copies = [
        pltpu.make_async_copy(source, loaded_sea if f == M else loaded.at[f], sems.at[f])
        for f, source in enumerate(sources)
    ]
    for copy in copies:
        copy.start()

    for f in range(FIELDS):
        copies[f].wait()
        source = loaded_sea if f == M else loaded.at[f]
        first_cols = jnp.zeros((8, LANES), jnp.float32)
        last_cols = first_cols
        for r in range(ROWS):
            begin = OWN_LANE + COLS * r
            here = (lane >= begin) & (lane < begin + COLS)
            for k in range(tiles):
                value = source[pl.ds(8 * k + r, 8, stride=8 * tiles), :].astype(jnp.float32)
                own[f, r, :, pl.ds(k * LANES, LANES)] = value
                if k == 0:
                    first_cols = jnp.where(here, turn(value, begin), first_cols)
                if k == tiles - 1:
                    last_cols = jnp.where(here, turn(value, begin + COLS), last_cols)
        firsts[f] = first_cols
        lasts[f] = last_cols
        swap_even[f] = jnp.where(even, last_cols, first_cols)
        swap_odd[f] = jnp.where(even, first_cols, last_cols)


def border_kernel(own, swap_even, swap_odd, coef, state, kept):
    tiles = own.shape[-1] // LANES

    def put(item, k, value):
        for which, items in enumerate((TO_NORTH, TO_SOUTH)):
            if item in items:
                kept[which, items.index(item) * tiles + k] = value

    def get(f, r, k):
        return own[f, r, :, pl.ds(k * LANES, LANES)]

    for f in range(FIELDS):
        for r in range(ROWS):
            for k in range(tiles):
                put((0, f, r), k, get(f, r, k))

    closed = [(jnp.zeros((8, LANES), jnp.float32),) * 2] * tiles
    faces = [closed] + [north_faces(get, r, tiles) for r in range(ROWS - 1)] + [closed]
    for r in range(ROWS):
        for k in range(tiles):
            for i in range(2):
                put((FACE, i, r), k, faces[r + 1][k][i])
    for begin in range(0, ROWS, BORDER_GROUP):
        rows = range(begin, begin + BORDER_GROUP)
        weights = weights_of(get, rows, tiles, faces[begin + 1 :], faces[begin:])
        for r in rows:
            for k in range(tiles):
                for i in range(7):
                    coef[i, r, :, pl.ds(k * LANES, LANES)] = weights[r - begin][k][i]

    for n in range(3):
        def read(t, r, k, n=n):
            return get(t, r, k) if n == 0 else state[n - 1, t, r, :, pl.ds(k * LANES, LANES)]

        for r in range(n, ROWS - n):
            if n == 2 and r not in (n, ROWS - 1 - n):
                continue
            for k in range(tiles):
                cols = pl.ds(k * LANES, LANES)
                weights = [coef[i, r, :, cols] for i in range(7)]
                for t in range(2):
                    value = read(t, r, k)
                    to_north = read(t, r + 1, k) if r + 1 < ROWS - n else 0.0
                    to_south = read(t, r - 1, k) if r > n else 0.0
                    stepped = stencil(
                        weights,
                        value,
                        east(value, read(t, r, k + 1)) if k + 1 < tiles else turn(value, -1),
                        west(value, read(t, r, k - 1)) if k else turn(value, 1),
                        to_north,
                        to_south,
                    )
                    if r == n:
                        if n:
                            stepped = stepped + coef[3, r - 1, :, cols] * value
                        put((PART, t, r), k, stepped)
                    elif r == ROWS - 1 - n:
                        if n:
                            stepped = stepped + coef[4, r + 1, :, cols] * value
                        put((PART, t, r), k, stepped)
                    else:
                        state[n, t, r, :, cols] = stepped
                        put((n + 1, t, r), k, stepped)

    even = is_even("merid")

    @pl.when(even)
    def _():
        swap_even[...] = kept[0]
        swap_odd[...] = kept[1]

    @pl.when(jnp.logical_not(even))
    def _():
        swap_even[...] = kept[1]
        swap_odd[...] = kept[0]


def strips_kernel(firsts, lasts, zonal_even, zonal_odd, swap_even, swap_odd):
    lane = lanes()
    even = is_even("merid")
    even_zonal = is_even("zonal")
    for f in range(FIELDS):
        from_east = jnp.where(even_zonal, zonal_even[f], zonal_odd[f])
        from_west = jnp.where(even_zonal, zonal_odd[f], zonal_even[f])
        messages = []
        for pieces in (STRIPS_TO_NORTH, STRIPS_TO_SOUTH):
            message = jnp.zeros((8, LANES), jnp.float32)
            for strip, (begin, length, there, _) in zip(
                (firsts[f], lasts[f], from_east, from_west), pieces
            ):
                moved = turn(strip, there - begin)
                message = jnp.where((lane >= there) & (lane < there + length), moved, message)
            messages.append(message)
        swap_even[f] = jnp.where(even, messages[0], messages[1])
        swap_odd[f] = jnp.where(even, messages[1], messages[0])


def solve_kernel(
    own, rows_even, rows_odd, firsts, lasts, zonal_even, zonal_odd, strips_even, strips_odd,
    out, field, coef, state, part,
):
    tiles = own.shape[-1] // LANES
    lane = lanes()
    column = lax.rem(lane, COLS)
    at_first = column == 0
    at_last = column == COLS - 1

    even = is_even("merid")
    even_zonal = is_even("zonal")

    def cols(k):
        return pl.ds(k * LANES, LANES)

    def unpack(source, items, offset):
        for i, (n, f, r) in enumerate(items):
            e = r + offset + BORDER
            for k in range(tiles):
                value = source[i * tiles + k]
                if n == FACE:
                    coef[3 + f, e, :, cols(k)] = value
                elif n == PART:
                    part[f, e, :, cols(k)] = value
                elif f < 2:
                    state[n % 2, f, e, :, cols(k)] = value
                else:
                    field[f, e, :, cols(k)] = value

    @pl.when(even)
    def _():
        unpack(rows_odd, TO_NORTH, -ROWS)
        unpack(rows_even, TO_SOUTH, ROWS)

    @pl.when(jnp.logical_not(even))
    def _():
        unpack(rows_even, TO_NORTH, -ROWS)
        unpack(rows_odd, TO_SOUTH, ROWS)

    def assembled(which, source):
        fields = []
        for f in range(FIELDS):
            value = source(f)
            strips_south = jnp.where(even, strips_odd[f], strips_even[f])
            strips_north = jnp.where(even, strips_even[f], strips_odd[f])
            for message, pieces in ((strips_south, STRIPS_TO_NORTH), (strips_north, STRIPS_TO_SOUTH)):
                _, length, there, begin = pieces[which]
                moved = turn(message, begin - there)
                value = jnp.where((lane >= begin) & (lane < begin + length), moved, value)
            fields.append(value)
        return fields

    own_first = assembled(0, lambda f: firsts[f])
    own_last = assembled(1, lambda f: lasts[f])
    east_first = assembled(2, lambda f: jnp.where(even_zonal, zonal_even[f], zonal_odd[f]))
    west_last = assembled(3, lambda f: jnp.where(even_zonal, zonal_odd[f], zonal_even[f]))

    def to_first(value):
        return turn(value, 1 - COLS)

    def to_last(value):
        return turn(value, COLS - 1)

    def strip_weights(left, right):
        both = left[M] * jnp.where(at_last, to_last(right[M]), turn(left[M], -1))
        left_faces = face(left[U], left[K], both)
        right_faces = face(right[U], right[K], right[M] * turn(right[M], -1))
        left_west = tuple(turn(v, 1) for v in left_faces)
        right_west = tuple(
            jnp.where(at_first, to_first(l), turn(v, 1)) for l, v in zip(left_faces, right_faces)
        )
        weights = []
        for strip, faces, faces_west in ((left, left_faces, left_west), (right, right_faces, right_west)):
            north = face(strip[V], strip[K], strip[M] * turn(strip[M], -COLS))
            south = tuple(turn(v, COLS) for v in north)
            weights.append(
                collected(strip[M], faces, faces_west, north, south, vertical(strip[KZ], strip[M]))
            )
        return weights[0], weights[1], left_faces

    w_west_last, w_own_first, west_face = strip_weights(west_last, own_first)
    w_own_last, w_east_first, east_face = strip_weights(own_last, east_first)

    def trace(value, ghost):
        return FACTOR_B * value - FACTOR_A * ghost

    def robin(told, value):
        return (told + FACTOR_A * value) * (1.0 / FACTOR_B)

    ghosts = [[], []]
    first_steps = [[], []]
    last_steps = [[], []]
    held = [
        (own_first[t], own_last[t], east_first[t], west_last[t], own_first[t], own_last[t])
        for t in range(2)
    ]
    constant = [(to_first(west_last[t]), to_last(east_first[t])) for t in range(2)]
    for n in range(STEPS):
        told = []
        for (a_first, a_last, *_), (ghost_first, ghost_last) in zip(held, constant):
            told.append(
                (to_first(trace(a_last, ghost_last)), to_last(trace(a_first, ghost_first)))
            )
        robins = []
        traces = []
        for (_, _, b_first, b_last, *_), (told_first, told_last) in zip(held, told):
            robins.append((robin(told_first, b_first), robin(told_last, b_last)))
            traces.append((trace(b_first, robins[-1][0]), trace(b_last, robins[-1][1])))
        for t in range(2):
            trace_first, trace_last = traces[t]
            ghosts[t].append(
                jnp.where(at_last, trace_last, turn(trace_first, COLS - 2)) * (1.0 / FACTOR_B)
            )
        steps = []
        for t in range(2):
            a_first, a_last, b_first, b_last, c_first, c_last = held[t]
            if n < STEPS - 1:
                steps += [
                    (w_own_first, a_first, constant[t][0], True),
                    (w_own_last, a_last, constant[t][1], False),
                    (w_east_first, b_first, robins[t][0], True),
                    (w_west_last, b_last, robins[t][1], False),
                ]
            if n < BORDER:
                steps += [
                    (w_own_first, c_first, robin(to_first(traces[t][1]), c_first), True),
                    (w_own_last, c_last, robin(to_last(traces[t][0]), c_last), False),
                ]
        turned = [
            (turn(v, -1), turn(v, 1), turn(v, -COLS), turn(v, COLS), upward(v), downward(v))
            for _, v, _, _ in steps
        ]
        stepped = []
        for (weights, value, ghost, is_first), (e, w, north, south, up, down) in zip(steps, turned):
            if is_first:
                w = jnp.where(at_first, ghost, w)
            else:
                e = jnp.where(at_last, ghost, e)
            stepped.append(weighted(weights, (value, e, w, north, south, up, down)))
        count = len(stepped) // 2
        for t in range(2):
            mine = stepped[t * count : (t + 1) * count]
            if n < BORDER:
                first_steps[t].append(mine[-2])
                last_steps[t].append(mine[-1])
            held[t] = tuple(mine) + (mine[0],) * (6 - count) if count else held[t]

    def ends_of(value, r):
        return turn(value, -(COLS * (r + RIM) + COLS - 1))

    faces_at_ends = [
        jnp.where(at_last, w, turn(e, -1)) for w, e in zip(west_face, east_face)
    ]

    def fixed(value, n, t, r, k):
        if n and k == 0:
            exact = turn(first_steps[t][n - 1], -COLS * (r + RIM))
            value = jnp.where(lane < n, exact, value)
        if n and k == tiles - 1:
            exact = turn(last_steps[t][n - 1], -COLS * (r + RIM + 1))
            value = jnp.where(lane >= LANES - n, exact, value)
        return value

    for n in (1, 2):
        for t in range(2):
            for r in (-1 - n, ROWS + n):
                for k in (0, tiles - 1):
                    value = state[n % 2, t, r + BORDER, :, cols(k)]
                    state[n % 2, t, r + BORDER, :, cols(k)] = fixed(value, n, t, r, k)

    def get(f, r, k):
        if 0 <= r < ROWS:
            return own[f, r, :, cols(k)]
        return field[f, r + BORDER, :, cols(k)]

    def read(n, t, r, k):
        if n == 0 and 0 <= r < ROWS:
            return own[t, r, :, cols(k)]
        return state[n % 2, t, r + BORDER, :, cols(k)]

    faces_south = []
    for k in range(tiles):
        here, there = (coef[i, 0, :, cols(k)] for i in (3, 4))
        faces_south.append((here, there))
        coef[3, 0, :, cols(k)] = -there
    reach = BORDER - 1
    for begin in range(-reach, ROWS + reach, GROUP):
        rows = range(begin, begin + GROUP)
        faces = [faces_south] + [north_faces(get, r, tiles) for r in rows]
        interfaces = [tuple(ends_of(v, r) for v in faces_at_ends) for r in rows]
        weights = weights_of(get, rows, tiles, faces[1:], faces[:-1], interfaces)
        faces_south = faces[-1]
        for r in rows:
            for k in range(tiles):
                for i in range(7):
                    coef[i, r + BORDER, :, cols(k)] = weights[r - begin][k][i]
    for k in range(tiles):
        coef[4, ROWS + reach + BORDER, :, cols(k)] = faces_south[k][0]

    for n in range(STEPS):
        if n < BORDER:
            for t in range(2):
                for k in range(tiles):
                    r = -1 - n
                    e = r + BORDER
                    stepped = (
                        part[t, e, :, cols(k)]
                        + coef[3, e, :, cols(k)] * read(n, t, r + 1, k)
                        - coef[4, e + 1, :, cols(k)] * read(n, t, r, k)
                    )
                    state[(n + 1) % 2, t, e, :, cols(k)] = fixed(stepped, n + 1, t, r, k)
                    r = ROWS + n
                    e = r + BORDER
                    stepped = (
                        part[t, e, :, cols(k)]
                        + coef[4, e, :, cols(k)] * read(n, t, r - 1, k)
                        - coef[3, e - 1, :, cols(k)] * read(n, t, r, k)
                    )
                    state[(n + 1) % 2, t, e, :, cols(k)] = fixed(stepped, n + 1, t, r, k)
        more = min(n, STEPS - 1 - n)
        for r in range(-more, ROWS + more):
            ends = [ends_of(ghosts[t][n], r) for t in range(2)]
            for k in range(tiles):
                weights = [coef[i, r + BORDER, :, cols(k)] for i in range(7)]
                for t in range(2):
                    value = read(n, t, r, k)
                    if k == 0 or k == tiles - 1:
                        ghost = ends[t] + (FACTOR_A / FACTOR_B) * value
                    if k == 0:
                        to_west = jnp.where(lane == 0, ghost, turn(value, 1))
                    else:
                        to_west = west(value, read(n, t, r, k - 1))
                    if k == tiles - 1:
                        to_east = jnp.where(lane == LANES - 1, ghost, turn(value, -1))
                    else:
                        to_east = east(value, read(n, t, r, k + 1))
                    stepped = stencil(
                        weights, value, to_east, to_west, read(n, t, r + 1, k), read(n, t, r - 1, k)
                    )
                    if n == STEPS - 1:
                        out[t, pl.ds(8 * k + r, 8, stride=8 * tiles), :] = stepped
                    else:
                        state[(n + 1) % 2, t, r + BORDER, :, cols(k)] = stepped


def granted(mib=16):
    return pltpu.CompilerParams(vmem_limit_bytes=mib * 1024 * 1024)


def work(flops):
    return pl.CostEstimate(flops=flops, bytes_accessed=0, transcendentals=0)


def in_vmem(count):
    return [pl.BlockSpec(memory_space=pltpu.VMEM)] * count


def in_tiles(array):
    lead = array.shape[:-2]
    tiled = array.reshape(lead + (8, -1, LANES))
    return jnp.swapaxes(tiled, -3, -2).reshape(lead[:-1] + (-1, LANES))


def from_tiles(array, shape):
    tiled = array.reshape(shape[:-2] + (-1, 8, LANES))
    return jnp.swapaxes(tiled, -3, -2).reshape(shape)


def pack(*arrays):
    f32 = jnp.float32
    width = arrays[1].size // 64
    return pl.pallas_call(
        pack_kernel,
        out_shape=(
            jax.ShapeDtypeStruct((FIELDS, ROWS, 8, width), f32),
        )
        + (jax.ShapeDtypeStruct((FIELDS, 8, LANES), f32),) * 4,
        in_specs=[pl.BlockSpec(memory_space=pltpu.HBM)] * 6,
        out_specs=tuple(in_vmem(5)),
        scratch_shapes=[
            pltpu.VMEM((M,) + arrays[1].shape, f32),
            pltpu.VMEM(arrays[5].shape, arrays[5].dtype),
            pltpu.SemaphoreType.DMA((FIELDS,)),
        ],
        compiler_params=granted(),
        name="pack",
    )(*arrays)


def border(own):
    f32 = jnp.float32
    width = own.shape[-1]
    message = (UNITS * width // LANES, 8, LANES)
    return pl.pallas_call(
        border_kernel,
        out_shape=(jax.ShapeDtypeStruct(message, f32),) * 2,
        in_specs=in_vmem(1),
        out_specs=tuple(in_vmem(2)),
        scratch_shapes=[
            pltpu.VMEM((7, ROWS, 8, width), f32),
            pltpu.VMEM((2, 2, ROWS, 8, width), f32),
            pltpu.VMEM((2,) + message, f32),
        ],
        compiler_params=granted(),
        name="border",
    )(own)


def exchange_strips(*strips):
    shape = jax.ShapeDtypeStruct((FIELDS, 8, LANES), jnp.float32)
    return pl.pallas_call(
        strips_kernel,
        out_shape=(shape, shape),
        in_specs=in_vmem(4),
        out_specs=tuple(in_vmem(2)),
        compiler_params=granted(),
        cost_estimate=work(100_000_000_000),
        name="strips",
    )(*strips)


def solve(own, *others):
    f32 = jnp.float32
    width = own.shape[-1]
    rows = ROWS + 2 * BORDER
    return pl.pallas_call(
        solve_kernel,
        out_shape=jax.ShapeDtypeStruct((2, width // LANES * 64, LANES), f32),
        in_specs=in_vmem(9),
        out_specs=in_vmem(1)[0],
        scratch_shapes=[
            pltpu.VMEM((FIELDS, rows, 8, width), f32),
            pltpu.VMEM((7, rows, 8, width), f32),
            pltpu.VMEM((2, 2, rows, 8, width), f32),
            pltpu.VMEM((2, rows, 8, width), f32),
        ],
        compiler_params=granted(),
        name="solve",
    )(own, *others)


def swapped(axis, arrays, periodic):
    count = lax.axis_size(axis)
    received = []
    for start, array in enumerate(arrays):
        pairs = [(i, (i + 1) % count) for i in range(start, count, 2) if periodic or i + 1 < count]
        received.append(lax.ppermute(array, axis, pairs + [(b, a) for a, b in pairs]))
    return received


def shards(tracers, speed_east, speed_north, diff_horiz, diff_vert, sea_mask):
    arrays = (tracers, speed_east, speed_north, diff_horiz, diff_vert, sea_mask)
    own, firsts, lasts, *zonal = pack(
        *[pltpu.with_memory_space_constraint(in_tiles(a), pltpu.HBM) for a in arrays]
    )
    zonal = swapped("zonal", zonal, True)
    rows = swapped("merid", border(own), False)
    strips = swapped("merid", exchange_strips(firsts, lasts, *zonal), False)
    result = solve(own, *rows, firsts, lasts, *zonal, *strips)
    return from_tiles(result, tracers.shape)


def solution(mesh):
    row = P(None, "merid", "zonal")
    whole = P(None, None, "merid", "zonal")
    return jax.shard_map(
        shards, mesh=mesh, in_specs=(whole, row, row, row, row, row), out_specs=whole, check_vma=False
    )
```

```python
import jax
import jax.numpy as jnp
from jax import lax
from jax.experimental import pallas as pl
from jax.experimental.pallas import tpu as pltpu
from jax.sharding import PartitionSpec as P

STEPS = 6
LANES = 128
ROWS = 8

ROBIN_WEIGHT = 0.5
FACTOR_A = 1.0 - ROBIN_WEIGHT / 2.0
FACTOR_B = 1.0 + ROBIN_WEIGHT / 2.0

U, V, K, KZ, M = 2, 3, 4, 5, 6
FIELDS = 7

PART, FACE = 3, 4
TO_SOUTH = (
    [(n, t, n) for t in (0, 1) for n in (0, 1, 2)]
    + [(PART, t, n) for t in (0, 1) for n in (0, 1, 2)]
    + [(0, f, r) for f in (U, V, K, KZ) for r in (0, 1)]
    + [(0, M, r) for r in (0, 1, 2)]
)
TO_NORTH = (
    [(n, t, 7 - n) for t in (0, 1) for n in (0, 1, 2)]
    + [(PART, t, 7 - n) for t in (0, 1) for n in (0, 1, 2)]
    + [(0, f, r) for f in (U, V, K, KZ, M) for r in (6, 7)]
    + [(FACE, i, 5) for i in (0, 1)]
)
UNITS = max(len(TO_SOUTH), len(TO_NORTH))
BORDER = 3
BORDER_GROUP = 4

COLS = 6
RIM = 6
OWN_LANE = COLS * RIM

STRIPS_TO_SOUTH = ((36, 33, 0, 84), (36, 36, 33, 84), (36, 25, 69, 84), (36, 30, 94, 84))
STRIPS_TO_NORTH = ((48, 36, 0, 0), (51, 33, 36, 3), (54, 30, 69, 6), (59, 25, 99, 11))


def lanes():
    return lax.broadcasted_iota(jnp.int32, (8, LANES), 1)


def is_even(axis):
    return lax.rem(lax.axis_index(axis), 2) == 0


def turn(value, shift):
    shift = shift % LANES
    return pltpu.roll(value, shift, 1) if shift else value


def upward(value):
    return pltpu.roll(value, 7, 0)


def downward(value):
    return pltpu.roll(value, 1, 0)


def west(value, beside):
    return turn(jnp.where(lanes() == LANES - 1, beside, value), 1)


def east(value, beside):
    return turn(jnp.where(lanes() == 0, beside, value), -1)


def face(speed, diff, both):
    return (jnp.maximum(speed, 0.0) + diff) * both, (jnp.minimum(speed, 0.0) - diff) * both


def vertical(diff, sea):
    level = lax.broadcasted_iota(jnp.int32, (8, LANES), 0)
    below = diff * sea * jnp.where(level == 7, 0.0, upward(sea))
    return below, downward(below)


def collected(sea, faces_east, faces_west, faces_north, faces_south, faces_vertical):
    here, there = faces_east
    here_west, there_west = faces_west
    north_here, north_there = faces_north
    south_here, south_there = faces_south
    below, above = faces_vertical
    centre = sea - ((here - there_west) + (north_here - south_there) + (below + above))
    return centre, -there, here_west, -north_there, south_here, below, above


def weighted(weights, values):
    centre, w_east, w_west, w_north, w_south, w_below, w_above = weights
    value, to_east, to_west, to_north, to_south, below, above = values
    return (
        (centre * value + (w_north * to_north + w_south * to_south))
        + (w_below * below + w_above * above)
        + (w_east * to_east + w_west * to_west)
    )


def stencil(weights, value, to_east, to_west, to_north, to_south):
    values = (value, to_east, to_west, to_north, to_south, upward(value), downward(value))
    return weighted(weights, values)


def north_faces(get, r, tiles):
    return [
        face(get(V, r, k), get(K, r, k), get(M, r, k) * get(M, r + 1, k)) for k in range(tiles)
    ]


def strip_columns():
    column = lax.rem(lanes(), COLS)
    return column == 0, column == COLS - 1


def to_first(value):
    return turn(value, 1 - COLS)


def to_last(value):
    return turn(value, COLS - 1)


def left_faces(left, right):
    _, at_last = strip_columns()
    both = left[M] * jnp.where(at_last, to_last(right[M]), turn(left[M], -1))
    return face(left[U], left[K], both)


def faces_of_ends(west_face, east_face):
    _, at_last = strip_columns()
    return [jnp.where(at_last, w, turn(e, -1)) for w, e in zip(west_face, east_face)]


def ends_of(value, r):
    return turn(value, -(COLS * (r + RIM) + COLS - 1))


def weights_of(get, rows, tiles, faces_north, faces_south, interfaces=None):
    lane = lanes()
    cells = [(r, k) for r in rows for k in range(tiles)]
    sea = {(r, k): get(M, r, k) for r, k in cells}
    beside = {
        (r, k): east(sea[r, k], sea[r, k + 1]) if k + 1 < tiles else turn(sea[r, k], -1) for r, k in cells
    }
    beneath = {c: upward(sea[c]) for c in cells}
    bottom = lax.broadcasted_iota(jnp.int32, (8, LANES), 0) == 7
    faces, below = {}, {}
    for c in cells:
        faces[c] = face(get(U, *c), get(K, *c), sea[c] * beside[c])
        below[c] = get(KZ, *c) * sea[c] * jnp.where(bottom, 0.0, beneath[c])
    before = {}
    for i, r in enumerate(rows):
        ends = faces[r, tiles - 1]
        if interfaces is not None:
            at_end = lane == LANES - 1
            faces[r, tiles - 1] = tuple(
                jnp.where(at_end, turned, end) for turned, end in zip(interfaces[i], ends)
            )
            ends = tuple(turn(v, -1) for v in interfaces[i])
        before[r] = ends
    above = {c: downward(below[c]) for c in cells}
    faces_west = {}
    for r, k in cells:
        others = faces[r, k - 1] if k else before[r]
        faces_west[r, k] = tuple(west(v, b) for v, b in zip(faces[r, k], others))
    return [
        [
            collected(
                sea[r, k], faces[r, k], faces_west[r, k], faces_north[i][k], faces_south[i][k],
                (below[r, k], above[r, k]),
            )
            for k in range(tiles)
        ]
        for i, r in enumerate(rows)
    ]


def pack_kernel(
    tracers, speed_east, speed_north, diff_horiz, diff_vert, sea,
    own, firsts, lasts, swap_even, swap_odd, loaded, loaded_sea, sems,
):
    tiles = own.shape[-1] // LANES
    even = is_even("zonal")
    lane = lanes()
    sources = (tracers.at[0], tracers.at[1], speed_east, speed_north, diff_horiz, diff_vert, sea)
    copies = [
        pltpu.make_async_copy(source, loaded_sea if f == M else loaded.at[f], sems.at[f])
        for f, source in enumerate(sources)
    ]
    for copy in copies:
        copy.start()

    for copy in copies:
        copy.wait()
    for f in range(FIELDS):
        source = loaded_sea if f == M else loaded.at[f]
        first_cols = jnp.zeros((8, LANES), jnp.float32)
        last_cols = first_cols
        for r in range(ROWS):
            begin = OWN_LANE + COLS * r
            here = (lane >= begin) & (lane < begin + COLS)
            for k in range(tiles):
                value = source[pl.ds(8 * k + r, 8, stride=8 * tiles), :].astype(jnp.float32)
                own[f, r, :, pl.ds(k * LANES, LANES)] = value
                if k == 0:
                    first_cols = jnp.where(here, turn(value, begin), first_cols)
                if k == tiles - 1:
                    last_cols = jnp.where(here, turn(value, begin + COLS), last_cols)
        firsts[f] = first_cols
        lasts[f] = last_cols
        swap_even[f] = jnp.where(even, last_cols, first_cols)
        swap_odd[f] = jnp.where(even, first_cols, last_cols)


def border_kernel(own, swap_even, swap_odd, coef, state, kept):
    tiles = own.shape[-1] // LANES

    def put(item, k, value):
        for which, items in enumerate((TO_NORTH, TO_SOUTH)):
            if item in items:
                kept[which, items.index(item) * tiles + k] = value

    def get(f, r, k):
        return own[f, r, :, pl.ds(k * LANES, LANES)]

    for f in range(FIELDS):
        for r in range(ROWS):
            for k in range(tiles):
                put((0, f, r), k, get(f, r, k))

    closed = [(jnp.zeros((8, LANES), jnp.float32),) * 2] * tiles
    faces = [closed] + [north_faces(get, r, tiles) for r in range(ROWS - 1)] + [closed]
    for r in range(ROWS):
        for k in range(tiles):
            for i in range(2):
                put((FACE, i, r), k, faces[r + 1][k][i])
    for begin in range(0, ROWS, BORDER_GROUP):
        rows = range(begin, begin + BORDER_GROUP)
        weights = weights_of(get, rows, tiles, faces[begin + 1 :], faces[begin:])
        for r in rows:
            for k in range(tiles):
                for i in range(7):
                    coef[i, r, :, pl.ds(k * LANES, LANES)] = weights[r - begin][k][i]

    for n in range(3):
        def read(t, r, k, n=n):
            return get(t, r, k) if n == 0 else state[n - 1, t, r, :, pl.ds(k * LANES, LANES)]

        for r in range(n, ROWS - n):
            if n == 2 and r not in (n, ROWS - 1 - n):
                continue
            for k in range(tiles):
                cols = pl.ds(k * LANES, LANES)
                weights = [coef[i, r, :, cols] for i in range(7)]
                for t in range(2):
                    value = read(t, r, k)
                    to_north = read(t, r + 1, k) if r + 1 < ROWS - n else 0.0
                    to_south = read(t, r - 1, k) if r > n else 0.0
                    stepped = stencil(
                        weights,
                        value,
                        east(value, read(t, r, k + 1)) if k + 1 < tiles else turn(value, -1),
                        west(value, read(t, r, k - 1)) if k else turn(value, 1),
                        to_north,
                        to_south,
                    )
                    if r == n:
                        if n:
                            stepped = stepped + coef[3, r - 1, :, cols] * value
                        put((PART, t, r), k, stepped)
                    elif r == ROWS - 1 - n:
                        if n:
                            stepped = stepped + coef[4, r + 1, :, cols] * value
                        put((PART, t, r), k, stepped)
                    else:
                        state[n, t, r, :, cols] = stepped
                        put((n + 1, t, r), k, stepped)

    even = is_even("merid")

    @pl.when(even)
    def _():
        swap_even[...] = kept[0]
        swap_odd[...] = kept[1]

    @pl.when(jnp.logical_not(even))
    def _():
        swap_even[...] = kept[1]
        swap_odd[...] = kept[0]


def strips_kernel(firsts, lasts, zonal_even, zonal_odd, swap_even, swap_odd):
    lane = lanes()
    even = is_even("merid")
    even_zonal = is_even("zonal")
    for f in range(FIELDS):
        from_east = jnp.where(even_zonal, zonal_even[f], zonal_odd[f])
        from_west = jnp.where(even_zonal, zonal_odd[f], zonal_even[f])
        messages = []
        for pieces in (STRIPS_TO_NORTH, STRIPS_TO_SOUTH):
            message = jnp.zeros((8, LANES), jnp.float32)
            for strip, (begin, length, there, _) in zip(
                (firsts[f], lasts[f], from_east, from_west), pieces
            ):
                moved = turn(strip, there - begin)
                message = jnp.where((lane >= there) & (lane < there + length), moved, message)
            messages.append(message)
        swap_even[f] = jnp.where(even, messages[0], messages[1])
        swap_odd[f] = jnp.where(even, messages[1], messages[0])


def inner_kernel(own, firsts, lasts, zonal_even, zonal_odd, inner):
    tiles = own.shape[-1] // LANES
    even_zonal = is_even("zonal")
    from_east = [jnp.where(even_zonal, zonal_even[f], zonal_odd[f]) for f in range(FIELDS)]
    from_west = [jnp.where(even_zonal, zonal_odd[f], zonal_even[f]) for f in range(FIELDS)]
    faces_at_ends = faces_of_ends(left_faces(from_west, firsts), left_faces(lasts, from_east))

    def get(f, r, k):
        return own[f, r, :, pl.ds(k * LANES, LANES)]

    rows = range(1, ROWS - 1)
    north = [north_faces(get, r, tiles) for r in range(ROWS - 1)]
    interfaces = [tuple(ends_of(v, r) for v in faces_at_ends) for r in rows]
    weights = weights_of(get, rows, tiles, north[1:], north[:-1], interfaces)
    for r, row in zip(rows, weights):
        for k in range(tiles):
            for i in range(7):
                inner[i, r - 1, :, pl.ds(k * LANES, LANES)] = row[k][i]


def solve_kernel(
    own, inner, rows_even, rows_odd, firsts, lasts, zonal_even, zonal_odd, strips_even, strips_odd,
    out, field, coef, state, part,
):
    tiles = own.shape[-1] // LANES
    lane = lanes()
    column = lax.rem(lane, COLS)
    at_first = column == 0
    at_last = column == COLS - 1

    even = is_even("merid")
    even_zonal = is_even("zonal")

    def cols(k):
        return pl.ds(k * LANES, LANES)

    def unpack(source, items, offset):
        for i, (n, f, r) in enumerate(items):
            e = r + offset + BORDER
            for k in range(tiles):
                value = source[i * tiles + k]
                if n == FACE:
                    coef[3 + f, e, :, cols(k)] = value
                elif n == PART:
                    part[f, e, :, cols(k)] = value
                elif f < 2:
                    state[n % 2, f, e, :, cols(k)] = value
                else:
                    field[f, e, :, cols(k)] = value

    @pl.when(even)
    def _():
        unpack(rows_odd, TO_NORTH, -ROWS)
        unpack(rows_even, TO_SOUTH, ROWS)

    @pl.when(jnp.logical_not(even))
    def _():
        unpack(rows_even, TO_NORTH, -ROWS)
        unpack(rows_odd, TO_SOUTH, ROWS)

    def assembled(which, source):
        fields = []
        for f in range(FIELDS):
            value = source(f)
            strips_south = jnp.where(even, strips_odd[f], strips_even[f])
            strips_north = jnp.where(even, strips_even[f], strips_odd[f])
            for message, pieces in ((strips_south, STRIPS_TO_NORTH), (strips_north, STRIPS_TO_SOUTH)):
                _, length, there, begin = pieces[which]
                moved = turn(message, begin - there)
                value = jnp.where((lane >= begin) & (lane < begin + length), moved, value)
            fields.append(value)
        return fields

    own_first = assembled(0, lambda f: firsts[f])
    own_last = assembled(1, lambda f: lasts[f])
    east_first = assembled(2, lambda f: jnp.where(even_zonal, zonal_even[f], zonal_odd[f]))
    west_last = assembled(3, lambda f: jnp.where(even_zonal, zonal_odd[f], zonal_even[f]))

    def strip_weights(left, right):
        faces_left = left_faces(left, right)
        right_faces = face(right[U], right[K], right[M] * turn(right[M], -1))
        left_west = tuple(turn(v, 1) for v in faces_left)
        right_west = tuple(
            jnp.where(at_first, to_first(l), turn(v, 1)) for l, v in zip(faces_left, right_faces)
        )
        weights = []
        for strip, faces, faces_west in ((left, faces_left, left_west), (right, right_faces, right_west)):
            north = face(strip[V], strip[K], strip[M] * turn(strip[M], -COLS))
            south = tuple(turn(v, COLS) for v in north)
            weights.append(
                collected(strip[M], faces, faces_west, north, south, vertical(strip[KZ], strip[M]))
            )
        return weights[0], weights[1], faces_left

    w_west_last, w_own_first, west_face = strip_weights(west_last, own_first)
    w_own_last, w_east_first, east_face = strip_weights(own_last, east_first)

    def trace(value, ghost):
        return FACTOR_B * value - FACTOR_A * ghost

    def robin(told, value):
        return (told + FACTOR_A * value) * (1.0 / FACTOR_B)

    ghosts = [[], []]
    first_steps = [[], []]
    last_steps = [[], []]
    held = [
        (own_first[t], own_last[t], east_first[t], west_last[t], own_first[t], own_last[t])
        for t in range(2)
    ]
    constant = [(to_first(west_last[t]), to_last(east_first[t])) for t in range(2)]
    for n in range(STEPS):
        told = []
        for (a_first, a_last, *_), (ghost_first, ghost_last) in zip(held, constant):
            told.append(
                (to_first(trace(a_last, ghost_last)), to_last(trace(a_first, ghost_first)))
            )
        robins = []
        traces = []
        for (_, _, b_first, b_last, *_), (told_first, told_last) in zip(held, told):
            robins.append((robin(told_first, b_first), robin(told_last, b_last)))
            traces.append((trace(b_first, robins[-1][0]), trace(b_last, robins[-1][1])))
        for t in range(2):
            trace_first, trace_last = traces[t]
            ghosts[t].append(
                jnp.where(at_last, trace_last, turn(trace_first, COLS - 2)) * (1.0 / FACTOR_B)
            )
        steps = []
        for t in range(2):
            a_first, a_last, b_first, b_last, c_first, c_last = held[t]
            if n < STEPS - 1:
                steps += [
                    (w_own_first, a_first, constant[t][0], True),
                    (w_own_last, a_last, constant[t][1], False),
                    (w_east_first, b_first, robins[t][0], True),
                    (w_west_last, b_last, robins[t][1], False),
                ]
            if n < BORDER:
                steps += [
                    (w_own_first, c_first, robin(to_first(traces[t][1]), c_first), True),
                    (w_own_last, c_last, robin(to_last(traces[t][0]), c_last), False),
                ]
        turned = [
            (turn(v, -1), turn(v, 1), turn(v, -COLS), turn(v, COLS), upward(v), downward(v))
            for _, v, _, _ in steps
        ]
        stepped = []
        for (weights, value, ghost, is_first), (e, w, north, south, up, down) in zip(steps, turned):
            if is_first:
                w = jnp.where(at_first, ghost, w)
            else:
                e = jnp.where(at_last, ghost, e)
            stepped.append(weighted(weights, (value, e, w, north, south, up, down)))
        count = len(stepped) // 2
        for t in range(2):
            mine = stepped[t * count : (t + 1) * count]
            if n < BORDER:
                first_steps[t].append(mine[-2])
                last_steps[t].append(mine[-1])
            held[t] = tuple(mine) + (mine[0],) * (6 - count) if count else held[t]

    faces_at_ends = faces_of_ends(west_face, east_face)

    def fixed(value, n, t, r, k):
        if n and k == 0:
            exact = turn(first_steps[t][n - 1], -COLS * (r + RIM))
            value = jnp.where(lane < n, exact, value)
        if n and k == tiles - 1:
            exact = turn(last_steps[t][n - 1], -COLS * (r + RIM + 1))
            value = jnp.where(lane >= LANES - n, exact, value)
        return value

    for n in (1, 2):
        for t in range(2):
            for r in (-1 - n, ROWS + n):
                for k in (0, tiles - 1):
                    value = state[n % 2, t, r + BORDER, :, cols(k)]
                    state[n % 2, t, r + BORDER, :, cols(k)] = fixed(value, n, t, r, k)

    def get(f, r, k):
        if 0 <= r < ROWS:
            return own[f, r, :, cols(k)]
        return field[f, r + BORDER, :, cols(k)]

    def read(n, t, r, k):
        if n == 0 and 0 <= r < ROWS:
            return own[t, r, :, cols(k)]
        return state[n % 2, t, r + BORDER, :, cols(k)]

    faces_south = []
    for k in range(tiles):
        here, there = (coef[i, 0, :, cols(k)] for i in (3, 4))
        faces_south.append((here, there))
        coef[3, 0, :, cols(k)] = -there
    reach = BORDER - 1
    rows = [*range(-reach, 1), *range(ROWS - 1, ROWS + reach)]
    north = {r: north_faces(get, r, tiles) for r in rows + [ROWS - 2]}
    weights = weights_of(
        get, rows, tiles, [north[r] for r in rows],
        [north[r - 1] if r > -reach else faces_south for r in rows],
        [tuple(ends_of(v, r) for v in faces_at_ends) for r in rows],
    )
    for r, row in zip(rows, weights):
        for k in range(tiles):
            for i in range(7):
                coef[i, r + BORDER, :, cols(k)] = row[k][i]
    for k in range(tiles):
        coef[4, ROWS + reach + BORDER, :, cols(k)] = north[rows[-1]][k][0]

    def weight(i, r, k):
        if 0 < r < ROWS - 1:
            return inner[i, r - 1, :, cols(k)]
        return coef[i, r + BORDER, :, cols(k)]

    for n in range(STEPS):
        if n < BORDER:
            for t in range(2):
                for k in range(tiles):
                    r = -1 - n
                    e = r + BORDER
                    stepped = (
                        part[t, e, :, cols(k)]
                        + coef[3, e, :, cols(k)] * read(n, t, r + 1, k)
                        - coef[4, e + 1, :, cols(k)] * read(n, t, r, k)
                    )
                    state[(n + 1) % 2, t, e, :, cols(k)] = fixed(stepped, n + 1, t, r, k)
                    r = ROWS + n
                    e = r + BORDER
                    stepped = (
                        part[t, e, :, cols(k)]
                        + coef[4, e, :, cols(k)] * read(n, t, r - 1, k)
                        - coef[3, e - 1, :, cols(k)] * read(n, t, r, k)
                    )
                    state[(n + 1) % 2, t, e, :, cols(k)] = fixed(stepped, n + 1, t, r, k)
        more = min(n, STEPS - 1 - n)
        for r in range(-more, ROWS + more):
            ends = [ends_of(ghosts[t][n], r) for t in range(2)]
            for k in range(tiles):
                weights = [weight(i, r, k) for i in range(7)]
                for t in range(2):
                    value = read(n, t, r, k)
                    if k == 0 or k == tiles - 1:
                        ghost = ends[t] + (FACTOR_A / FACTOR_B) * value
                    if k == 0:
                        to_west = jnp.where(lane == 0, ghost, turn(value, 1))
                    else:
                        to_west = west(value, read(n, t, r, k - 1))
                    if k == tiles - 1:
                        to_east = jnp.where(lane == LANES - 1, ghost, turn(value, -1))
                    else:
                        to_east = east(value, read(n, t, r, k + 1))
                    stepped = stencil(
                        weights, value, to_east, to_west, read(n, t, r + 1, k), read(n, t, r - 1, k)
                    )
                    if n == STEPS - 1:
                        out[t, pl.ds(8 * k + r, 8, stride=8 * tiles), :] = stepped
                    else:
                        state[(n + 1) % 2, t, r + BORDER, :, cols(k)] = stepped


def granted(mib=16):
    return pltpu.CompilerParams(vmem_limit_bytes=mib * 1024 * 1024)


def work(flops):
    return pl.CostEstimate(flops=flops, bytes_accessed=0, transcendentals=0)


def in_vmem(count):
    return [pl.BlockSpec(memory_space=pltpu.VMEM)] * count


def in_tiles(array):
    lead = array.shape[:-2]
    tiled = array.reshape(lead + (8, -1, LANES))
    return jnp.swapaxes(tiled, -3, -2).reshape(lead[:-1] + (-1, LANES))


def from_tiles(array, shape):
    tiled = array.reshape(shape[:-2] + (-1, 8, LANES))
    return jnp.swapaxes(tiled, -3, -2).reshape(shape)


def pack(*arrays):
    f32 = jnp.float32
    width = arrays[1].size // 64
    return pl.pallas_call(
        pack_kernel,
        out_shape=(
            jax.ShapeDtypeStruct((FIELDS, ROWS, 8, width), f32),
        )
        + (jax.ShapeDtypeStruct((FIELDS, 8, LANES), f32),) * 4,
        in_specs=[pl.BlockSpec(memory_space=pltpu.HBM)] * 6,
        out_specs=tuple(in_vmem(5)),
        scratch_shapes=[
            pltpu.VMEM((M,) + arrays[1].shape, f32),
            pltpu.VMEM(arrays[5].shape, arrays[5].dtype),
            pltpu.SemaphoreType.DMA((FIELDS,)),
        ],
        compiler_params=granted(),
        name="pack",
    )(*arrays)


def border(own):
    f32 = jnp.float32
    width = own.shape[-1]
    message = (UNITS * width // LANES, 8, LANES)
    return pl.pallas_call(
        border_kernel,
        out_shape=(jax.ShapeDtypeStruct(message, f32),) * 2,
        in_specs=in_vmem(1),
        out_specs=tuple(in_vmem(2)),
        scratch_shapes=[
            pltpu.VMEM((7, ROWS, 8, width), f32),
            pltpu.VMEM((2, 2, ROWS, 8, width), f32),
            pltpu.VMEM((2,) + message, f32),
        ],
        compiler_params=granted(),
        name="border",
    )(own)


def exchange_strips(*strips):
    shape = jax.ShapeDtypeStruct((FIELDS, 8, LANES), jnp.float32)
    return pl.pallas_call(
        strips_kernel,
        out_shape=(shape, shape),
        in_specs=in_vmem(4),
        out_specs=tuple(in_vmem(2)),
        compiler_params=granted(),
        cost_estimate=work(100_000_000_000),
        name="strips",
    )(*strips)


def weigh_inner(own, *strips):
    return pl.pallas_call(
        inner_kernel,
        out_shape=jax.ShapeDtypeStruct((7, ROWS - 2, 8, own.shape[-1]), jnp.float32),
        in_specs=in_vmem(5),
        out_specs=in_vmem(1)[0],
        compiler_params=granted(),
        cost_estimate=work(1_000_000_000),
        name="inner",
    )(own, *strips)


def solve(own, *others):
    f32 = jnp.float32
    width = own.shape[-1]
    rows = ROWS + 2 * BORDER
    return pl.pallas_call(
        solve_kernel,
        out_shape=jax.ShapeDtypeStruct((2, width // LANES * 64, LANES), f32),
        in_specs=in_vmem(10),
        out_specs=in_vmem(1)[0],
        scratch_shapes=[
            pltpu.VMEM((FIELDS, rows, 8, width), f32),
            pltpu.VMEM((7, rows, 8, width), f32),
            pltpu.VMEM((2, 2, rows, 8, width), f32),
            pltpu.VMEM((2, rows, 8, width), f32),
        ],
        compiler_params=granted(),
        name="solve",
    )(own, *others)


def swapped(axis, arrays, periodic):
    count = lax.axis_size(axis)
    received = []
    for start, array in enumerate(arrays):
        pairs = [(i, (i + 1) % count) for i in range(start, count, 2) if periodic or i + 1 < count]
        received.append(lax.ppermute(array, axis, pairs + [(b, a) for a, b in pairs]))
    return received


def shards(tracers, speed_east, speed_north, diff_horiz, diff_vert, sea_mask):
    arrays = (tracers, speed_east, speed_north, diff_horiz, diff_vert, sea_mask)
    own, firsts, lasts, *zonal = pack(
        *[pltpu.with_memory_space_constraint(in_tiles(a), pltpu.HBM) for a in arrays]
    )
    zonal = swapped("zonal", zonal, True)
    rows = swapped("merid", border(own), False)
    strips = swapped("merid", exchange_strips(firsts, lasts, *zonal), False)
    inner = weigh_inner(own, firsts, lasts, *zonal)
    result = solve(own, inner, *rows, firsts, lasts, *zonal, *strips)
    return from_tiles(result, tracers.shape)


def solution(mesh):
    row = P(None, "merid", "zonal")
    whole = P(None, None, "merid", "zonal")
    return jax.shard_map(
        shards, mesh=mesh, in_specs=(whole, row, row, row, row, row), out_specs=whole, check_vma=False
    )
```

```python
import jax
import jax.numpy as jnp
from jax import lax
from jax.experimental import pallas as pl
from jax.experimental.pallas import tpu as pltpu
from jax.sharding import PartitionSpec as P

STEPS = 6
LANES = 128
ROWS = 8

ROBIN_WEIGHT = 0.5
FACTOR_A = 1.0 - ROBIN_WEIGHT / 2.0
FACTOR_B = 1.0 + ROBIN_WEIGHT / 2.0

U, V, K, KZ, M = 2, 3, 4, 5, 6
FIELDS = 7

PART, FACE = 3, 4
TO_SOUTH = (
    [(n, t, n) for t in (0, 1) for n in (0, 1, 2)]
    + [(PART, t, n) for t in (0, 1) for n in (0, 1, 2)]
    + [(0, f, r) for f in (U, V, K, KZ) for r in (0, 1)]
    + [(0, M, r) for r in (0, 1, 2)]
)
TO_NORTH = (
    [(n, t, 7 - n) for t in (0, 1) for n in (0, 1, 2)]
    + [(PART, t, 7 - n) for t in (0, 1) for n in (0, 1, 2)]
    + [(0, f, r) for f in (U, V, K, KZ, M) for r in (6, 7)]
    + [(FACE, i, 5) for i in (0, 1)]
)
UNITS = max(len(TO_SOUTH), len(TO_NORTH))
BORDER = 3
BORDER_GROUP = 4

COLS = 6
RIM = 6
OWN_LANE = COLS * RIM

STRIPS_TO_SOUTH = ((36, 33, 0, 84), (36, 36, 33, 84), (36, 25, 69, 84), (36, 30, 94, 84))
STRIPS_TO_NORTH = ((48, 36, 0, 0), (51, 33, 36, 3), (54, 30, 69, 6), (59, 25, 99, 11))


def lanes():
    return lax.broadcasted_iota(jnp.int32, (8, LANES), 1)


def is_even(axis):
    return lax.rem(lax.axis_index(axis), 2) == 0


def turn(value, shift):
    shift = shift % LANES
    return pltpu.roll(value, shift, 1) if shift else value


def upward(value):
    return pltpu.roll(value, 7, 0)


def downward(value):
    return pltpu.roll(value, 1, 0)


def west(value, beside):
    return turn(jnp.where(lanes() == LANES - 1, beside, value), 1)


def east(value, beside):
    return turn(jnp.where(lanes() == 0, beside, value), -1)


def face(speed, diff, both):
    return (jnp.maximum(speed, 0.0) + diff) * both, (jnp.minimum(speed, 0.0) - diff) * both


def vertical(diff, sea):
    level = lax.broadcasted_iota(jnp.int32, (8, LANES), 0)
    below = diff * sea * jnp.where(level == 7, 0.0, upward(sea))
    return below, downward(below)


def collected(sea, faces_east, faces_west, faces_north, faces_south, faces_vertical):
    here, there = faces_east
    here_west, there_west = faces_west
    north_here, north_there = faces_north
    south_here, south_there = faces_south
    below, above = faces_vertical
    centre = sea - ((here - there_west) + (north_here - south_there) + (below + above))
    return centre, -there, here_west, -north_there, south_here, below, above


def weighted(weights, values):
    centre, w_east, w_west, w_north, w_south, w_below, w_above = weights
    value, to_east, to_west, to_north, to_south, below, above = values
    return (
        (centre * value + (w_north * to_north + w_south * to_south))
        + (w_below * below + w_above * above)
        + (w_east * to_east + w_west * to_west)
    )


def stencil(weights, value, to_east, to_west, to_north, to_south):
    values = (value, to_east, to_west, to_north, to_south, upward(value), downward(value))
    return weighted(weights, values)


def north_faces(get, r, tiles):
    return [
        face(get(V, r, k), get(K, r, k), get(M, r, k) * get(M, r + 1, k)) for k in range(tiles)
    ]


def strip_columns():
    column = lax.rem(lanes(), COLS)
    return column == 0, column == COLS - 1


def to_first(value):
    return turn(value, 1 - COLS)


def to_last(value):
    return turn(value, COLS - 1)


def left_faces(left, right):
    _, at_last = strip_columns()
    both = left[M] * jnp.where(at_last, to_last(right[M]), turn(left[M], -1))
    return face(left[U], left[K], both)


def faces_of_ends(west_face, east_face):
    _, at_last = strip_columns()
    return [jnp.where(at_last, w, turn(e, -1)) for w, e in zip(west_face, east_face)]


def ends_of(value, r):
    return turn(value, -(COLS * (r + RIM) + COLS - 1))


def weights_of(get, rows, tiles, faces_north, faces_south, interfaces=None):
    lane = lanes()
    cells = [(r, k) for r in rows for k in range(tiles)]
    sea = {(r, k): get(M, r, k) for r, k in cells}
    beside = {
        (r, k): east(sea[r, k], sea[r, k + 1]) if k + 1 < tiles else turn(sea[r, k], -1) for r, k in cells
    }
    beneath = {c: upward(sea[c]) for c in cells}
    bottom = lax.broadcasted_iota(jnp.int32, (8, LANES), 0) == 7
    faces, below = {}, {}
    for c in cells:
        faces[c] = face(get(U, *c), get(K, *c), sea[c] * beside[c])
        below[c] = get(KZ, *c) * sea[c] * jnp.where(bottom, 0.0, beneath[c])
    before = {}
    for i, r in enumerate(rows):
        ends = faces[r, tiles - 1]
        if interfaces is not None:
            at_end = lane == LANES - 1
            faces[r, tiles - 1] = tuple(
                jnp.where(at_end, turned, end) for turned, end in zip(interfaces[i], ends)
            )
            ends = tuple(turn(v, -1) for v in interfaces[i])
        before[r] = ends
    above = {c: downward(below[c]) for c in cells}
    faces_west = {}
    for r, k in cells:
        others = faces[r, k - 1] if k else before[r]
        faces_west[r, k] = tuple(west(v, b) for v, b in zip(faces[r, k], others))
    return [
        [
            collected(
                sea[r, k], faces[r, k], faces_west[r, k], faces_north[i][k], faces_south[i][k],
                (below[r, k], above[r, k]),
            )
            for k in range(tiles)
        ]
        for i, r in enumerate(rows)
    ]


def pack_kernel(
    tracers, speed_east, speed_north, diff_horiz, diff_vert, sea,
    own, firsts, lasts, swap_even, swap_odd, loaded, loaded_sea, sems,
):
    tiles = own.shape[-1] // LANES
    even = is_even("zonal")
    lane = lanes()
    sources = (tracers.at[0], tracers.at[1], speed_east, speed_north, diff_horiz, diff_vert, sea)
    copies = [
        pltpu.make_async_copy(source, loaded_sea if f == M else loaded.at[f], sems.at[f])
        for f, source in enumerate(sources)
    ]
    for copy in copies:
        copy.start()

    for copy in copies:
        copy.wait()
    for f in range(FIELDS):
        source = loaded_sea if f == M else loaded.at[f]
        first_cols = jnp.zeros((8, LANES), jnp.float32)
        last_cols = first_cols
        for r in range(ROWS):
            begin = OWN_LANE + COLS * r
            here = (lane >= begin) & (lane < begin + COLS)
            for k in range(tiles):
                value = source[pl.ds(8 * k + r, 8, stride=8 * tiles), :].astype(jnp.float32)
                own[f, r, :, pl.ds(k * LANES, LANES)] = value
                if k == 0:
                    first_cols = jnp.where(here, turn(value, begin), first_cols)
                if k == tiles - 1:
                    last_cols = jnp.where(here, turn(value, begin + COLS), last_cols)
        firsts[f] = first_cols
        lasts[f] = last_cols
        swap_even[f] = jnp.where(even, last_cols, first_cols)
        swap_odd[f] = jnp.where(even, first_cols, last_cols)


def border_kernel(own, swap_even, swap_odd, coef, state, kept):
    tiles = own.shape[-1] // LANES

    def put(item, k, value):
        for which, items in enumerate((TO_NORTH, TO_SOUTH)):
            if item in items:
                kept[which, items.index(item) * tiles + k] = value

    def get(f, r, k):
        return own[f, r, :, pl.ds(k * LANES, LANES)]

    for f in range(FIELDS):
        for r in range(ROWS):
            for k in range(tiles):
                put((0, f, r), k, get(f, r, k))

    closed = [(jnp.zeros((8, LANES), jnp.float32),) * 2] * tiles
    faces = [closed] + [north_faces(get, r, tiles) for r in range(ROWS - 1)] + [closed]
    for r in range(ROWS):
        for k in range(tiles):
            for i in range(2):
                put((FACE, i, r), k, faces[r + 1][k][i])
    for begin in range(0, ROWS, BORDER_GROUP):
        rows = range(begin, begin + BORDER_GROUP)
        weights = weights_of(get, rows, tiles, faces[begin + 1 :], faces[begin:])
        for r in rows:
            for k in range(tiles):
                for i in range(7):
                    coef[i, r, :, pl.ds(k * LANES, LANES)] = weights[r - begin][k][i]

    for n in range(3):
        def read(t, r, k, n=n):
            return get(t, r, k) if n == 0 else state[n - 1, t, r, :, pl.ds(k * LANES, LANES)]

        for r in range(n, ROWS - n):
            if n == 2 and r not in (n, ROWS - 1 - n):
                continue
            for k in range(tiles):
                cols = pl.ds(k * LANES, LANES)
                weights = [coef[i, r, :, cols] for i in range(7)]
                for t in range(2):
                    value = read(t, r, k)
                    to_north = read(t, r + 1, k) if r + 1 < ROWS - n else 0.0
                    to_south = read(t, r - 1, k) if r > n else 0.0
                    stepped = stencil(
                        weights,
                        value,
                        east(value, read(t, r, k + 1)) if k + 1 < tiles else turn(value, -1),
                        west(value, read(t, r, k - 1)) if k else turn(value, 1),
                        to_north,
                        to_south,
                    )
                    if r == n:
                        if n:
                            stepped = stepped + coef[3, r - 1, :, cols] * value
                        put((PART, t, r), k, stepped)
                    elif r == ROWS - 1 - n:
                        if n:
                            stepped = stepped + coef[4, r + 1, :, cols] * value
                        put((PART, t, r), k, stepped)
                    else:
                        state[n, t, r, :, cols] = stepped
                        put((n + 1, t, r), k, stepped)

    even = is_even("merid")

    @pl.when(even)
    def _():
        swap_even[...] = kept[0]
        swap_odd[...] = kept[1]

    @pl.when(jnp.logical_not(even))
    def _():
        swap_even[...] = kept[1]
        swap_odd[...] = kept[0]


def strips_kernel(firsts, lasts, zonal_even, zonal_odd, swap_even, swap_odd):
    lane = lanes()
    even = is_even("merid")
    even_zonal = is_even("zonal")
    for f in range(FIELDS):
        from_east = jnp.where(even_zonal, zonal_even[f], zonal_odd[f])
        from_west = jnp.where(even_zonal, zonal_odd[f], zonal_even[f])
        messages = []
        for pieces in (STRIPS_TO_NORTH, STRIPS_TO_SOUTH):
            message = jnp.zeros((8, LANES), jnp.float32)
            for strip, (begin, length, there, _) in zip(
                (firsts[f], lasts[f], from_east, from_west), pieces
            ):
                moved = turn(strip, there - begin)
                message = jnp.where((lane >= there) & (lane < there + length), moved, message)
            messages.append(message)
        swap_even[f] = jnp.where(even, messages[0], messages[1])
        swap_odd[f] = jnp.where(even, messages[1], messages[0])


def inner_kernel(own, firsts, lasts, zonal_even, zonal_odd, inner):
    tiles = own.shape[-1] // LANES
    even_zonal = is_even("zonal")
    from_east = [jnp.where(even_zonal, zonal_even[f], zonal_odd[f]) for f in range(FIELDS)]
    from_west = [jnp.where(even_zonal, zonal_odd[f], zonal_even[f]) for f in range(FIELDS)]
    faces_at_ends = faces_of_ends(left_faces(from_west, firsts), left_faces(lasts, from_east))

    def get(f, r, k):
        return own[f, r, :, pl.ds(k * LANES, LANES)]

    rows = range(1, ROWS - 1)
    north = [north_faces(get, r, tiles) for r in range(ROWS - 1)]
    interfaces = [tuple(ends_of(v, r) for v in faces_at_ends) for r in rows]
    weights = weights_of(get, rows, tiles, north[1:], north[:-1], interfaces)
    for r, row in zip(rows, weights):
        for k in range(tiles):
            for i in range(7):
                inner[i, r - 1, :, pl.ds(k * LANES, LANES)] = row[k][i]


def solve_kernel(
    own, inner, rows_even, rows_odd, firsts, lasts, zonal_even, zonal_odd, strips_even, strips_odd,
    out, field, coef, state, part, result, sems,
):
    tiles = own.shape[-1] // LANES
    lane = lanes()
    column = lax.rem(lane, COLS)
    at_first = column == 0
    at_last = column == COLS - 1

    even = is_even("merid")
    even_zonal = is_even("zonal")

    def cols(k):
        return pl.ds(k * LANES, LANES)

    def unpack(source, items, offset):
        for i, (n, f, r) in enumerate(items):
            e = r + offset + BORDER
            for k in range(tiles):
                value = source[i * tiles + k]
                if n == FACE:
                    coef[3 + f, e, :, cols(k)] = value
                elif n == PART:
                    part[f, e, :, cols(k)] = value
                elif f < 2:
                    state[n % 2, f, e, :, cols(k)] = value
                else:
                    field[f, e, :, cols(k)] = value

    @pl.when(even)
    def _():
        unpack(rows_odd, TO_NORTH, -ROWS)
        unpack(rows_even, TO_SOUTH, ROWS)

    @pl.when(jnp.logical_not(even))
    def _():
        unpack(rows_even, TO_NORTH, -ROWS)
        unpack(rows_odd, TO_SOUTH, ROWS)

    def assembled(which, source):
        fields = []
        for f in range(FIELDS):
            value = source(f)
            strips_south = jnp.where(even, strips_odd[f], strips_even[f])
            strips_north = jnp.where(even, strips_even[f], strips_odd[f])
            for message, pieces in ((strips_south, STRIPS_TO_NORTH), (strips_north, STRIPS_TO_SOUTH)):
                _, length, there, begin = pieces[which]
                moved = turn(message, begin - there)
                value = jnp.where((lane >= begin) & (lane < begin + length), moved, value)
            fields.append(value)
        return fields

    own_first = assembled(0, lambda f: firsts[f])
    own_last = assembled(1, lambda f: lasts[f])
    east_first = assembled(2, lambda f: jnp.where(even_zonal, zonal_even[f], zonal_odd[f]))
    west_last = assembled(3, lambda f: jnp.where(even_zonal, zonal_odd[f], zonal_even[f]))

    def strip_weights(left, right):
        faces_left = left_faces(left, right)
        right_faces = face(right[U], right[K], right[M] * turn(right[M], -1))
        left_west = tuple(turn(v, 1) for v in faces_left)
        right_west = tuple(
            jnp.where(at_first, to_first(l), turn(v, 1)) for l, v in zip(faces_left, right_faces)
        )
        weights = []
        for strip, faces, faces_west in ((left, faces_left, left_west), (right, right_faces, right_west)):
            north = face(strip[V], strip[K], strip[M] * turn(strip[M], -COLS))
            south = tuple(turn(v, COLS) for v in north)
            weights.append(
                collected(strip[M], faces, faces_west, north, south, vertical(strip[KZ], strip[M]))
            )
        return weights[0], weights[1], faces_left

    w_west_last, w_own_first, west_face = strip_weights(west_last, own_first)
    w_own_last, w_east_first, east_face = strip_weights(own_last, east_first)

    def trace(value, ghost):
        return FACTOR_B * value - FACTOR_A * ghost

    def robin(told, value):
        return (told + FACTOR_A * value) * (1.0 / FACTOR_B)

    ghosts = [[], []]
    first_steps = [[], []]
    last_steps = [[], []]
    held = [
        (own_first[t], own_last[t], east_first[t], west_last[t], own_first[t], own_last[t])
        for t in range(2)
    ]
    constant = [(to_first(west_last[t]), to_last(east_first[t])) for t in range(2)]
    for n in range(STEPS):
        told = []
        for (a_first, a_last, *_), (ghost_first, ghost_last) in zip(held, constant):
            told.append(
                (to_first(trace(a_last, ghost_last)), to_last(trace(a_first, ghost_first)))
            )
        robins = []
        traces = []
        for (_, _, b_first, b_last, *_), (told_first, told_last) in zip(held, told):
            robins.append((robin(told_first, b_first), robin(told_last, b_last)))
            traces.append((trace(b_first, robins[-1][0]), trace(b_last, robins[-1][1])))
        for t in range(2):
            trace_first, trace_last = traces[t]
            ghosts[t].append(
                jnp.where(at_last, trace_last, turn(trace_first, COLS - 2)) * (1.0 / FACTOR_B)
            )
        steps = []
        for t in range(2):
            a_first, a_last, b_first, b_last, c_first, c_last = held[t]
            if n < STEPS - 1:
                steps += [
                    (w_own_first, a_first, constant[t][0], True),
                    (w_own_last, a_last, constant[t][1], False),
                    (w_east_first, b_first, robins[t][0], True),
                    (w_west_last, b_last, robins[t][1], False),
                ]
            if n < BORDER:
                steps += [
                    (w_own_first, c_first, robin(to_first(traces[t][1]), c_first), True),
                    (w_own_last, c_last, robin(to_last(traces[t][0]), c_last), False),
                ]
        turned = [
            (turn(v, -1), turn(v, 1), turn(v, -COLS), turn(v, COLS), upward(v), downward(v))
            for _, v, _, _ in steps
        ]
        stepped = []
        for (weights, value, ghost, is_first), (e, w, north, south, up, down) in zip(steps, turned):
            if is_first:
                w = jnp.where(at_first, ghost, w)
            else:
                e = jnp.where(at_last, ghost, e)
            stepped.append(weighted(weights, (value, e, w, north, south, up, down)))
        count = len(stepped) // 2
        for t in range(2):
            mine = stepped[t * count : (t + 1) * count]
            if n < BORDER:
                first_steps[t].append(mine[-2])
                last_steps[t].append(mine[-1])
            held[t] = tuple(mine) + (mine[0],) * (6 - count) if count else held[t]

    faces_at_ends = faces_of_ends(west_face, east_face)

    def fixed(value, n, t, r, k):
        if n and k == 0:
            exact = turn(first_steps[t][n - 1], -COLS * (r + RIM))
            value = jnp.where(lane < n, exact, value)
        if n and k == tiles - 1:
            exact = turn(last_steps[t][n - 1], -COLS * (r + RIM + 1))
            value = jnp.where(lane >= LANES - n, exact, value)
        return value

    for n in (1, 2):
        for t in range(2):
            for r in (-1 - n, ROWS + n):
                for k in (0, tiles - 1):
                    value = state[n % 2, t, r + BORDER, :, cols(k)]
                    state[n % 2, t, r + BORDER, :, cols(k)] = fixed(value, n, t, r, k)

    def get(f, r, k):
        if 0 <= r < ROWS:
            return own[f, r, :, cols(k)]
        return field[f, r + BORDER, :, cols(k)]

    def read(n, t, r, k):
        if n == 0 and 0 <= r < ROWS:
            return own[t, r, :, cols(k)]
        return state[n % 2, t, r + BORDER, :, cols(k)]

    faces_south = []
    for k in range(tiles):
        here, there = (coef[i, 0, :, cols(k)] for i in (3, 4))
        faces_south.append((here, there))
        coef[3, 0, :, cols(k)] = -there
    reach = BORDER - 1
    rows = [*range(-reach, 1), *range(ROWS - 1, ROWS + reach)]
    north = {r: north_faces(get, r, tiles) for r in rows + [ROWS - 2]}
    weights = weights_of(
        get, rows, tiles, [north[r] for r in rows],
        [north[r - 1] if r > -reach else faces_south for r in rows],
        [tuple(ends_of(v, r) for v in faces_at_ends) for r in rows],
    )
    for r, row in zip(rows, weights):
        for k in range(tiles):
            for i in range(7):
                coef[i, r + BORDER, :, cols(k)] = row[k][i]
    for k in range(tiles):
        coef[4, ROWS + reach + BORDER, :, cols(k)] = north[rows[-1]][k][0]

    leaving = [pltpu.make_async_copy(result.at[t], out.at[t], sems.at[t]) for t in range(2)]

    def weight(i, r, k):
        if 0 < r < ROWS - 1:
            return inner[i, r - 1, :, cols(k)]
        return coef[i, r + BORDER, :, cols(k)]

    for n in range(STEPS):
        if n < BORDER:
            for t in range(2):
                for k in range(tiles):
                    r = -1 - n
                    e = r + BORDER
                    stepped = (
                        part[t, e, :, cols(k)]
                        + coef[3, e, :, cols(k)] * read(n, t, r + 1, k)
                        - coef[4, e + 1, :, cols(k)] * read(n, t, r, k)
                    )
                    state[(n + 1) % 2, t, e, :, cols(k)] = fixed(stepped, n + 1, t, r, k)
                    r = ROWS + n
                    e = r + BORDER
                    stepped = (
                        part[t, e, :, cols(k)]
                        + coef[4, e, :, cols(k)] * read(n, t, r - 1, k)
                        - coef[3, e - 1, :, cols(k)] * read(n, t, r, k)
                    )
                    state[(n + 1) % 2, t, e, :, cols(k)] = fixed(stepped, n + 1, t, r, k)
        more = min(n, STEPS - 1 - n)
        final = n == STEPS - 1
        turns = [(t,) for t in range(2)] if final else [(0, 1)]
        for tracers, r in [(ts, r) for ts in turns for r in range(-more, ROWS + more)]:
            ends = [ends_of(ghosts[t][n], r) for t in range(2)]
            for k in range(tiles):
                weights = [weight(i, r, k) for i in range(7)]
                for t in tracers:
                    value = read(n, t, r, k)
                    if k == 0 or k == tiles - 1:
                        ghost = ends[t] + (FACTOR_A / FACTOR_B) * value
                    if k == 0:
                        to_west = jnp.where(lane == 0, ghost, turn(value, 1))
                    else:
                        to_west = west(value, read(n, t, r, k - 1))
                    if k == tiles - 1:
                        to_east = jnp.where(lane == LANES - 1, ghost, turn(value, -1))
                    else:
                        to_east = east(value, read(n, t, r, k + 1))
                    stepped = stencil(
                        weights, value, to_east, to_west, read(n, t, r + 1, k), read(n, t, r - 1, k)
                    )
                    if final:
                        result[t, pl.ds(8 * k + r, 8, stride=8 * tiles), :] = stepped
                    else:
                        state[(n + 1) % 2, t, r + BORDER, :, cols(k)] = stepped
            if final and r == ROWS - 1:
                leaving[tracers[0]].start()
    for copy in leaving:
        copy.wait()


def granted(mib=16):
    return pltpu.CompilerParams(vmem_limit_bytes=mib * 1024 * 1024)


def work(flops):
    return pl.CostEstimate(flops=flops, bytes_accessed=0, transcendentals=0)


def in_vmem(count):
    return [pl.BlockSpec(memory_space=pltpu.VMEM)] * count


def in_tiles(array):
    lead = array.shape[:-2]
    tiled = array.reshape(lead + (8, -1, LANES))
    return jnp.swapaxes(tiled, -3, -2).reshape(lead[:-1] + (-1, LANES))


def from_tiles(array, shape):
    tiled = array.reshape(shape[:-2] + (-1, 8, LANES))
    return jnp.swapaxes(tiled, -3, -2).reshape(shape)


def pack(*arrays):
    f32 = jnp.float32
    width = arrays[1].size // 64
    return pl.pallas_call(
        pack_kernel,
        out_shape=(
            jax.ShapeDtypeStruct((FIELDS, ROWS, 8, width), f32),
        )
        + (jax.ShapeDtypeStruct((FIELDS, 8, LANES), f32),) * 4,
        in_specs=[pl.BlockSpec(memory_space=pltpu.HBM)] * 6,
        out_specs=tuple(in_vmem(5)),
        scratch_shapes=[
            pltpu.VMEM((M,) + arrays[1].shape, f32),
            pltpu.VMEM(arrays[5].shape, arrays[5].dtype),
            pltpu.SemaphoreType.DMA((FIELDS,)),
        ],
        compiler_params=granted(),
        name="pack",
    )(*arrays)


def border(own):
    f32 = jnp.float32
    width = own.shape[-1]
    message = (UNITS * width // LANES, 8, LANES)
    return pl.pallas_call(
        border_kernel,
        out_shape=(jax.ShapeDtypeStruct(message, f32),) * 2,
        in_specs=in_vmem(1),
        out_specs=tuple(in_vmem(2)),
        scratch_shapes=[
            pltpu.VMEM((7, ROWS, 8, width), f32),
            pltpu.VMEM((2, 2, ROWS, 8, width), f32),
            pltpu.VMEM((2,) + message, f32),
        ],
        compiler_params=granted(),
        name="border",
    )(own)


def exchange_strips(*strips):
    shape = jax.ShapeDtypeStruct((FIELDS, 8, LANES), jnp.float32)
    return pl.pallas_call(
        strips_kernel,
        out_shape=(shape, shape),
        in_specs=in_vmem(4),
        out_specs=tuple(in_vmem(2)),
        compiler_params=granted(),
        cost_estimate=work(100_000_000_000),
        name="strips",
    )(*strips)


def weigh_inner(own, *strips):
    return pl.pallas_call(
        inner_kernel,
        out_shape=jax.ShapeDtypeStruct((7, ROWS - 2, 8, own.shape[-1]), jnp.float32),
        in_specs=in_vmem(5),
        out_specs=in_vmem(1)[0],
        compiler_params=granted(),
        cost_estimate=work(1_000_000_000),
        name="inner",
    )(own, *strips)


def solve(own, *others):
    f32 = jnp.float32
    width = own.shape[-1]
    rows = ROWS + 2 * BORDER
    return pl.pallas_call(
        solve_kernel,
        out_shape=jax.ShapeDtypeStruct((2, width // LANES * 64, LANES), f32),
        in_specs=in_vmem(10),
        out_specs=pl.BlockSpec(memory_space=pltpu.HBM),
        scratch_shapes=[
            pltpu.VMEM((FIELDS, rows, 8, width), f32),
            pltpu.VMEM((7, rows, 8, width), f32),
            pltpu.VMEM((2, 2, rows, 8, width), f32),
            pltpu.VMEM((2, rows, 8, width), f32),
            pltpu.VMEM((2, width // LANES * 64, LANES), f32),
            pltpu.SemaphoreType.DMA((2,)),
        ],
        compiler_params=granted(),
        name="solve",
    )(own, *others)


def swapped(axis, arrays, periodic):
    count = lax.axis_size(axis)
    received = []
    for start, array in enumerate(arrays):
        pairs = [(i, (i + 1) % count) for i in range(start, count, 2) if periodic or i + 1 < count]
        received.append(lax.ppermute(array, axis, pairs + [(b, a) for a, b in pairs]))
    return received


def shards(tracers, speed_east, speed_north, diff_horiz, diff_vert, sea_mask):
    arrays = (tracers, speed_east, speed_north, diff_horiz, diff_vert, sea_mask)
    own, firsts, lasts, *zonal = pack(
        *[pltpu.with_memory_space_constraint(in_tiles(a), pltpu.HBM) for a in arrays]
    )
    zonal = swapped("zonal", zonal, True)
    rows = swapped("merid", border(own), False)
    strips = swapped("merid", exchange_strips(firsts, lasts, *zonal), False)
    inner = weigh_inner(own, firsts, lasts, *zonal)
    result = solve(own, inner, *rows, firsts, lasts, *zonal, *strips)
    return from_tiles(result, tracers.shape)


def solution(mesh):
    row = P(None, "merid", "zonal")
    whole = P(None, None, "merid", "zonal")
    return jax.shard_map(
        shards, mesh=mesh, in_specs=(whole, row, row, row, row, row), out_specs=whole, check_vma=False
    )
```
